512 devices in a mesh: dp: 2 (over core), fsdp: 16 (over x, y), tensor: 16 (over z).
Axes of the slice: x: 4, y: 4, z: 16, core: 2. Of those that a mesh axis runs over, the one named last changes fastest.
Arguments:
- momentum: bfloat16 [2, 8192, 14336], P('dp', 'fsdp', 'tensor'), may hold values from -40 to 40
- gradient: bfloat16 [2, 8192, 14336], P('dp', 'fsdp', 'tensor'), may hold values from -48 to 48
- right_factor: float32 [14336, 128], P('tensor'), may hold values from -0.046875 to 0.046875
Outputs:
- new_momentum: bfloat16 [2, 8192, 14336], P('dp', 'fsdp', 'tensor')
- update: bfloat16 [8192, 14336], P('fsdp', 'tensor')
- new_factor: float32 [14336, 128], P('tensor')
The draws below stay inside these ranges and needn't reach their ends.
All inputs are finite; a program needn't handle non-finite values.
Results may differ from the reference program's by a relative error of at most 0.012.
Values may be sent and summed in bfloat16 or wider, within the bound.
A program may use at most 64 MiB of HBM per device.

```python
import math
import jax
import jax.numpy as jnp
from jax import lax

D = 8192
FF = 14336
RANK = 128
ITERS = 2
REPLICAS = 2


def field_scales(key):
    row_key = jax.random.fold_in(key, 11)
    col_key = jax.random.fold_in(key, 12)
    rows = 3.0 ** (jnp.arange(D, dtype=jnp.float32) / D) * jnp.exp(jax.random.uniform(row_key, (D,), jnp.float32, 0.0, math.log(2.0)))
    cols = 3.0 ** (jnp.arange(FF, dtype=jnp.float32) / FF) * jnp.exp(jax.random.uniform(col_key, (FF,), jnp.float32, 0.0, math.log(3.4)))
    return 0.12 * rows[:, None] * cols[None, :]


def draw_momentum(key, part):
    scale = field_scales(key)
    key = jax.random.fold_in(key, 1)
    noise = jnp.clip(jax.random.normal(key, (REPLICAS, D, FF), jnp.float32), -4.0, 4.0)
    return (noise * scale[None]).astype(jnp.bfloat16)


def draw_gradient(key, part):
    scale = field_scales(key)
    key = jax.random.fold_in(key, 2)
    common_key, own_key = jax.random.split(key)
    common = jnp.clip(jax.random.normal(common_key, (D, FF), jnp.float32), -4.0, 4.0)
    own = jnp.clip(jax.random.normal(own_key, (REPLICAS, D, FF), jnp.float32), -4.0, 4.0)
    mixed = 0.7 * common[None] + 0.7 * own
    return (mixed * scale[None]).astype(jnp.bfloat16)


def shard_levels(rng, shape, cuts, low, largest):
    gain = 1.0
    for position, parts in cuts:
        heights = jax.random.uniform(jax.random.fold_in(jax.random.fold_in(rng, 6), position), (parts,), jnp.float32, low / len(cuts), largest / len(cuts))
        gain = gain * jnp.repeat(jnp.exp(heights), shape[position] // parts).reshape((-1,) + (1,) * (len(shape) - 1 - position))
    return gain


def scatter_about(stream_key, extent, scale, bound, pieces=(), held_as=jnp.bfloat16):
    gain = shard_levels(stream_key, extent, pieces, -0.22, 0.18) if pieces else 1.0
    entries = jax.random.normal(stream_key, extent, jnp.float32) * scale * gain
    return jnp.minimum(jnp.maximum(entries, -bound), bound).astype(held_as)


def setup_inputs(seed: int = 0) -> dict:
    splits = jax.random.split(jax.random.key(seed), 4)
    return {
        "momentum": draw_momentum(jax.random.fold_in(splits[3], 71), 0),
        "gradient": draw_gradient(jax.random.fold_in(splits[3], 71), 0),
        "right_factor": scatter_about(splits[2], (FF, RANK), FF ** -0.5, 0.046875, ((0, 16),), jnp.float32),
    }


def reference(momentum, gradient, right_factor):
    buffer = (momentum.astype(jnp.float32) + gradient.astype(jnp.float32)).astype(jnp.bfloat16)
    factor_b = right_factor.astype(jnp.bfloat16)
    ortho_b = None
    right = None
    new_factor = right_factor
    for step in range(ITERS):
        left = jnp.zeros((D, RANK), jnp.float32)
        for replica in range(REPLICAS):
            left = left + jnp.dot(buffer[replica].astype(jnp.float32), factor_b.astype(jnp.float32), preferred_element_type=jnp.float32)
        left = left / REPLICAS
        gram = jnp.dot(left.T, left, precision=lax.Precision.HIGHEST)
        lower = jnp.linalg.cholesky(gram)
        ortho_b = lax.linalg.triangular_solve(lower, left, left_side=False, lower=True, transpose_a=True).astype(jnp.bfloat16)
        right = jnp.zeros((FF, RANK), jnp.float32)
        for replica in range(REPLICAS):
            right = right + jnp.dot(buffer[replica].T.astype(jnp.float32), ortho_b.astype(jnp.float32), preferred_element_type=jnp.float32)
        right = right / REPLICAS
        squares = lax.optimization_barrier(jnp.sum(right * right, axis=0))
        new_factor = right / jnp.sqrt(squares + 1e-06)
        factor_b = new_factor.astype(jnp.bfloat16)
    right_b = right.astype(jnp.bfloat16)
    feedback = jnp.dot(ortho_b.astype(jnp.float32), right_b.T.astype(jnp.float32), preferred_element_type=jnp.float32)
    new_momentum = (buffer.astype(jnp.float32) - 0.05 * feedback[None]).astype(jnp.bfloat16)
    scale_value = math.sqrt(D * FF / RANK)
    update = (scale_value * jnp.dot(ortho_b.astype(jnp.float32), factor_b.T.astype(jnp.float32), preferred_element_type=jnp.float32)).astype(jnp.bfloat16)
    return (new_momentum, update, new_factor)
```

```python
import math

import jax
import jax.numpy as jnp
from jax import lax
from jax.experimental import pallas as pl
from jax.experimental.pallas import tpu as pltpu
from jax.sharding import PartitionSpec as P

D = 8192
FF = 14336
RANK = 128
MESH = pl.DeviceIdType.MESH
F32 = jnp.float32
BF16 = jnp.bfloat16
HIGHEST = lax.Precision.HIGHEST

NZ = 16
NXY = 16
GROUP = 32
ROWS = 512
HALF = 256
COLS = 896
XCH = HALF // NZ
WCH = 32
WOWN = COLS // WCH
TILES = COLS // 128
GCH = 8
NB = 16


def ring_offsets():
    return sorted(range(1, NZ), key=lambda d: -min(d, NZ - d))


def group_offsets():
    offs = [(dc, dx, dy) for dc in range(2) for dx in range(4) for dy in range(4)]
    offs.remove((0, 0, 0))
    return sorted(offs, key=lambda o: -(min(o[1], 4 - o[1]) + min(o[2], 4 - o[2])))


def split3(a):
    high = a.astype(BF16)
    rest = a - high.astype(F32)
    mid = rest.astype(BF16)
    low = (rest - mid.astype(F32)).astype(BF16)
    return high, mid, low


def outer_f32(u, v):
    u1, u2, u3 = split3(u)
    v1, v2, v3 = split3(v)
    left = jnp.concatenate([u1, u1, u2, u1, u2, u3], 0)
    right = jnp.concatenate([v1, v2, v1, v3, v2, v1], 0)
    return lax.dot_general(left, right, (((0,), (0,)), ((), ())), preferred_element_type=F32)


def inverse_cholesky(a_ref, e_ref):
    rows = lax.broadcasted_iota(jnp.int32, (RANK, RANK), 0)
    cols = lax.broadcasted_iota(jnp.int32, (RANK, RANK), 1)
    e_ref[...] = jnp.where(rows == cols, 1.0, 0.0).astype(F32)
    sub = lax.broadcasted_iota(jnp.int32, (NB, RANK), 0)

    def spread(t, j):
        return jnp.broadcast_to(t[j : j + 1, :], (NB, RANK))

    for base in range(0, RANK, NB):
        xa = a_ref[base : base + NB, :]
        xe = e_ref[base : base + NB, :]
        col = [
            jnp.broadcast_to(xa[:, base + k : base + k + 1], (NB, RANK)) for k in range(NB)
        ]
        va, ve, out = [], [], []
        for j in range(NB):
            pivot = spread(col[j], j)
            inv = 1.0 / pivot
            row_e = spread(xe, j)
            out.append((row_e * lax.rsqrt(pivot))[0:1])
            row_a = inv * spread(xa, j)
            row_e = inv * row_e
            va.append(row_a[0:1])
            ve.append(row_e[0:1])
            if j + 1 < NB:
                below = jnp.where(sub > j, col[j], 0.0)
                xa = xa - below * row_a
                xe = xe - below * row_e
                for k in range(j + 1, NB):
                    col[k] = col[k] - below * (inv * spread(col[k], j))
        last = base + NB
        if last < RANK:
            v = jnp.concatenate([jnp.concatenate(va, 0), jnp.concatenate(ve, 0)], 1)
            change = outer_f32(xa, v)
            a_ref[last:, :] = a_ref[last:, :] - change[last:, :RANK]
            e_ref[last:, :] = e_ref[last:, :] - change[last:, RANK:]
        e_ref[base:last, :] = jnp.concatenate(out, 0)


def right_times(tiles_ref, m):
    parts = jnp.concatenate(split3(m), 0)
    out = []
    for i in range(TILES):
        tile = tiles_ref[i * 128 : (i + 1) * 128, :]
        r = lax.dot_general(tile, parts, (((0,), (1,)), ((), ())), preferred_element_type=F32)
        out.append(r[:, :RANK] + (r[:, RANK : 2 * RANK] + r[:, 2 * RANK :]))
    return out


def rows_times(x, m):
    r = lax.dot_general(
        x, jnp.concatenate(split3(m), 0), (((1,), (1,)), ((), ())), preferred_element_type=F32
    )
    return r[:, :RANK] + (r[:, RANK : 2 * RANK] + r[:, 2 * RANK :])


def kernel(
    mom, grad, fac, new_mom, update, new_fac,
    m_v, g_v, f_v, fb, own, oth, xs, xr, xo, xa, xoth, ws, wr, wo, wa, gs, gr, go, ga,
    qs, qr, lower, a_s, right, ob, nm_v, up_v, nf_v, load, send, recv, store,
):
    c = lax.axis_index("dp")
    f = lax.axis_index("fsdp")
    t = lax.axis_index("tensor")
    x = f // 4
    y = lax.rem(f, 4)
    me = f * 2 + c
    other = 1 - c
    ring = [(c, f, lax.rem(t + d, NZ)) for d in ring_offsets()]
    group = []
    for dc, dx, dy in group_offsets():
        qf = lax.rem(x + dx, 4) * 4 + lax.rem(y + dy, 4)
        group.append((c if dc == 0 else other, qf, t))
    partner = (other, f, t)
    owner_w = me < WOWN
    owner_g = c == lax.rem(f, 2)

    def put(src, dst, phase, to):
        pltpu.make_async_remote_copy(
            src_ref=src, dst_ref=dst, send_sem=send.at[phase], recv_sem=recv.at[phase],
            device_id=to, device_id_type=MESH,
        ).start()

    def got(region, phase):
        pltpu.make_async_remote_copy(
            src_ref=region, dst_ref=region, send_sem=send.at[phase], recv_sem=recv.at[phase],
            device_id=partner, device_id_type=MESH,
        ).wait_recv()

    def sent(region, phase):
        pltpu.make_async_remote_copy(
            src_ref=region, dst_ref=region, send_sem=send.at[phase], recv_sem=recv.at[phase],
            device_id=partner, device_id_type=MESH,
        ).wait_send()

    barrier = pltpu.get_barrier_semaphore()
    for to in ring + group:
        pl.semaphore_signal(barrier, inc=1, device_id=to, device_id_type=MESH)

    starts = [pl.multiple_of(lax.rem(other * HALF + 128 * i, ROWS), 128) for i in range(4)]
    loads = []
    for i in range(4):
        r = pl.ds(starts[i], 128)
        pair = [
            pltpu.make_async_copy(mom.at[0, r], m_v.at[r], load.at[2 * i]),
            pltpu.make_async_copy(grad.at[0, r], g_v.at[r], load.at[2 * i + 1]),
        ]
        for copy in pair:
            copy.start()
        loads.append(pair)
    load_f = pltpu.make_async_copy(fac, f_v, load.at[8])
    load_f.start()
    for i in range(4):
        for copy in loads[i]:
            copy.wait()
        r = pl.ds(starts[i], 128)
        own[r, :] = (m_v[r, :].astype(F32) + g_v[r, :].astype(F32)).astype(BF16)
    load_f.wait()
    fb[...] = f_v[...].astype(BF16)

    mine = pl.ds(pl.multiple_of(c * HALF, HALF), HALF)
    theirs = pl.ds(pl.multiple_of(other * HALF, HALF), HALF)
    pl.semaphore_wait(barrier, len(ring) + len(group))

    put(own.at[theirs], oth, 0, partner)

    def left_out(it, acc):
        base = 2 + 7 * it
        xs[it] = (0.5 * acc).astype(BF16)
        for to in ring:
            src = xs.at[it, pl.ds(pl.multiple_of(to[2] * XCH, XCH), XCH)]
            put(src, xr.at[it, pl.ds(pl.multiple_of(t * XCH, XCH), XCH)], base, to)
        rows = pl.ds(pl.multiple_of(t * XCH, XCH), XCH)
        xr[it, rows, :] = xs[it, rows, :]

    def left_owned(it):
        got(xr.at[it, pl.ds(0, HALF - XCH)], 2 + 7 * it)
        total = xr[it, 0:XCH, :].astype(F32)
        for k in range(1, NZ):
            total = total + xr[it, k * XCH : (k + 1) * XCH, :].astype(F32)
        return total

    def left_spread(it, total):
        rows = pl.ds(pl.multiple_of(t * XCH, XCH), XCH)
        xo[it] = total.astype(BF16)
        for to in ring:
            put(xo.at[it], xa.at[it, rows], 3 + 7 * it, to)
        xa[it, rows, :] = total.astype(BF16)

    def left_here(it):
        got(xa.at[it, pl.ds(0, HALF - XCH)], 3 + 7 * it)
        return xa[it]

    def right_out(it, left):
        base = 4 + 7 * it
        dims = (((0,), (0,)), ((), ()))
        part = lax.dot_general(left, own[mine, :], dims, preferred_element_type=F32)
        part = part + lax.dot_general(left, oth[...], dims, preferred_element_type=F32)
        part = (0.5 * part).astype(BF16)
        for i in range(TILES):
            ws[it, i * 128 : (i + 1) * 128, :] = part[:, i * 128 : (i + 1) * 128]
        dst = wr.at[it, pl.ds(pl.multiple_of(me * WCH, WCH), WCH)]
        for to in group:
            q = to[1] * 2 + to[0]

            @pl.when(q < WOWN)
            def _():
                put(ws.at[it, pl.ds(pl.multiple_of(q * WCH, WCH), WCH)], dst, base, to)

        @pl.when(owner_w)
        def _():
            rows = pl.ds(pl.multiple_of(me * WCH, WCH), WCH)
            wr[it, rows, :] = ws[it, rows, :]

    def right_spread(it):
        @pl.when(owner_w)
        def _():
            got(wr.at[it, pl.ds(0, (GROUP - 1) * WCH)], 4 + 7 * it)
            total = wr[it, 0:WCH, :].astype(F32)
            for k in range(1, GROUP):
                total = total + wr[it, k * WCH : (k + 1) * WCH, :].astype(F32)
            wo[it] = total.astype(BF16)
            rows = pl.ds(pl.multiple_of(me * WCH, WCH), WCH)
            for to in group:
                put(wo.at[it], wa.at[it, rows], 5 + 7 * it, to)
            wa[it, rows, :] = total.astype(BF16)

    def right_here(it):
        @pl.when(owner_w)
        def _():
            got(wa.at[it, pl.ds(0, (WOWN - 1) * WCH)], 5 + 7 * it)

        @pl.when(jnp.logical_not(owner_w))
        def _():
            got(wa.at[it, pl.ds(0, WOWN * WCH)], 5 + 7 * it)

    def gram_out(it, left):
        dims = (((0,), (0,)), ((), ()))
        gs[it] = lax.dot_general(left, left, dims, preferred_element_type=F32)
        dst = gr.at[it, pl.ds(pl.multiple_of(me * GCH, GCH), GCH)]
        for to in group:

            @pl.when(to[0] == lax.rem(to[1], 2))
            def _():
                rows = pl.ds(pl.multiple_of(to[1] * GCH, GCH), GCH)
                put(gs.at[it, rows], dst, 6 + 7 * it, to)

        @pl.when(owner_g)
        def _():
            rows = pl.ds(pl.multiple_of(f * GCH, GCH), GCH)
            gr[it, pl.ds(pl.multiple_of(me * GCH, GCH), GCH), :] = gs[it, rows, :]

    def gram_spread(it):
        @pl.when(owner_g)
        def _():
            got(gr.at[it, pl.ds(0, (GROUP - 1) * GCH)], 6 + 7 * it)
            total = gr[it, 0:GCH, :]
            for k in range(1, GROUP):
                total = total + gr[it, k * GCH : (k + 1) * GCH, :]
            go[it] = total
            rows = pl.ds(pl.multiple_of(f * GCH, GCH), GCH)
            for to in group:
                put(go.at[it], ga.at[it, rows], 7 + 7 * it, to)
            ga[it, rows, :] = total

    def gram_here(it):
        @pl.when(owner_g)
        def _():
            got(ga.at[it, pl.ds(0, RANK - GCH)], 7 + 7 * it)

        @pl.when(jnp.logical_not(owner_g))
        def _():
            got(ga.at[it], 7 + 7 * it)

        return ga[it]

    def squares_out(it, tiles):
        total = jnp.sum(tiles[0] * tiles[0], axis=0, keepdims=True)
        for tile in tiles[1:]:
            total = total + jnp.sum(tile * tile, axis=0, keepdims=True)
        qs[it] = jnp.broadcast_to(total, (8, RANK))
        rows = pl.ds(pl.multiple_of(t * 8, 8), 8)
        for to in ring:
            put(qs.at[it], qr.at[it, rows], 8 + 7 * it, to)
        qr[it, rows, :] = qs[it]

    def norms(it):
        got(qr.at[it, pl.ds(0, (NZ - 1) * 8)], 8 + 7 * it)
        total = qr[it, 0:8, :]
        for k in range(1, NZ):
            total = total + qr[it, k * 8 : (k + 1) * 8, :]
        return jnp.sqrt(total[0:1, :] + 1e-06)

    part = jnp.dot(own[mine, :], fb[...], preferred_element_type=F32)
    got(oth, 0)
    left_out(0, part + jnp.dot(oth[...], fb[...], preferred_element_type=F32))
    left_spread(0, left_owned(0))
    left = left_here(0)
    right_out(0, left)
    gram_out(0, left)
    right_spread(0)
    gram_spread(0)
    right_here(0)

    factor_t = jnp.concatenate([wa[0, i * 128 : (i + 1) * 128, :] for i in range(TILES)], 1)
    nt = (((1,), (1,)), ((), ()))
    part = lax.dot_general(own[mine, :], factor_t, nt, preferred_element_type=F32)
    left_out(1, part + lax.dot_general(oth[...], factor_t, nt, preferred_element_type=F32))
    a_s[...] = gram_here(0)
    inverse_cholesky(a_s, lower.at[0])
    owned = left_owned(1)
    left_spread(
        1,
        lax.dot_general(owned, lower[0], nt, preferred_element_type=F32, precision=HIGHEST),
    )
    squares_out(0, right_times(wa.at[0], lower[0]))
    left = left_here(1)
    gram_out(1, left)
    right_out(1, left)
    put(xa.at[1], xoth, 1, partner)
    gram_spread(1)
    right_spread(1)
    scale = jnp.broadcast_to(1.0 / norms(0), (RANK, RANK))
    a_s[...] = gram_here(1) * scale * scale.T
    inverse_cholesky(a_s, lower.at[1])
    mix = lower[1] * scale
    got(xoth, 1)
    ob[mine, :] = rows_times(left, mix).astype(BF16)
    ob[theirs, :] = rows_times(xoth[...], mix).astype(BF16)
    right_here(1)
    tiles = right_times(wa.at[1], mix)
    squares_out(1, tiles)
    for i in range(TILES):
        right[i * 128 : (i + 1) * 128, :] = tiles[i]
    right_b = right[...].astype(BF16)
    outs = []
    for i in range(4):
        r = pl.ds(i * 128, 128)
        feedback = lax.dot_general(ob[r, :], right_b, nt, preferred_element_type=F32)
        nm_v[r, :] = (own[r, :].astype(F32) - 0.05 * feedback).astype(BF16)
        copy = pltpu.make_async_copy(nm_v.at[r], new_mom.at[0, r], store.at[i])
        copy.start()
        outs.append(copy)
    nf_v[...] = right[...] * (1.0 / norms(1))
    copy = pltpu.make_async_copy(nf_v, new_fac, store.at[8])
    copy.start()
    outs.append(copy)
    factor_b = nf_v[...].astype(BF16)
    for i in range(4):
        r = pl.ds(i * 128, 128)
        low_rank = lax.dot_general(ob[r, :], factor_b, nt, preferred_element_type=F32)
        up_v[r, :] = (math.sqrt(D * FF / RANK) * low_rank).astype(BF16)
        copy = pltpu.make_async_copy(up_v.at[r], update.at[r], store.at[4 + i])
        copy.start()
        outs.append(copy)

    sent(oth, 0)
    sent(xoth, 1)
    for it in range(2):
        sent(xs.at[it, pl.ds(0, HALF - XCH)], 2 + 7 * it)
        sent(xa.at[it, pl.ds(0, HALF - XCH)], 3 + 7 * it)

        @pl.when(owner_w)
        def _():
            sent(ws.at[it, pl.ds(0, (WOWN - 1) * WCH)], 4 + 7 * it)
            sent(wr.at[it, pl.ds(0, (GROUP - 1) * WCH)], 5 + 7 * it)

        @pl.when(jnp.logical_not(owner_w))
        def _():
            sent(ws.at[it, pl.ds(0, WOWN * WCH)], 4 + 7 * it)

        @pl.when(owner_g)
        def _():
            sent(gs.at[it, pl.ds(0, RANK - GCH)], 6 + 7 * it)
            sent(gr.at[it, pl.ds(0, (GROUP - 1) * GCH)], 7 + 7 * it)

        @pl.when(jnp.logical_not(owner_g))
        def _():
            sent(gs.at[it], 6 + 7 * it)

        sent(qr.at[it, pl.ds(0, (NZ - 1) * 8)], 8 + 7 * it)
    for copy in outs:
        copy.wait()


def shards(momentum, gradient, right_factor):
    scratch = [
        pltpu.VMEM((ROWS, COLS), BF16),
        pltpu.VMEM((ROWS, COLS), BF16),
        pltpu.VMEM((COLS, RANK), F32),
        pltpu.VMEM((COLS, RANK), BF16),
        pltpu.VMEM((ROWS, COLS), BF16),
        pltpu.VMEM((HALF, COLS), BF16),
        pltpu.VMEM((2, HALF, RANK), BF16),
        pltpu.VMEM((2, HALF, RANK), BF16),
        pltpu.VMEM((2, XCH, RANK), BF16),
        pltpu.VMEM((2, HALF, RANK), BF16),
        pltpu.VMEM((HALF, RANK), BF16),
        pltpu.VMEM((2, COLS, RANK), BF16),
        pltpu.VMEM((2, GROUP * WCH, RANK), BF16),
        pltpu.VMEM((2, WCH, RANK), BF16),
        pltpu.VMEM((2, COLS, RANK), BF16),
        pltpu.VMEM((2, RANK, RANK), F32),
        pltpu.VMEM((2, GROUP * GCH, RANK), F32),
        pltpu.VMEM((2, GCH, RANK), F32),
        pltpu.VMEM((2, RANK, RANK), F32),
        pltpu.VMEM((2, 8, RANK), F32),
        pltpu.VMEM((2, NZ * 8, RANK), F32),
        pltpu.VMEM((2, RANK, RANK), F32),
        pltpu.VMEM((RANK, RANK), F32),
        pltpu.VMEM((COLS, RANK), F32),
        pltpu.VMEM((ROWS, RANK), BF16),
        pltpu.VMEM((ROWS, COLS), BF16),
        pltpu.VMEM((ROWS, COLS), BF16),
        pltpu.VMEM((COLS, RANK), F32),
        pltpu.SemaphoreType.DMA((9,)),
        pltpu.SemaphoreType.DMA((16,)),
        pltpu.SemaphoreType.DMA((16,)),
        pltpu.SemaphoreType.DMA((9,)),
    ]
    anywhere = pl.BlockSpec(memory_space=pl.ANY)
    return pl.pallas_call(
        kernel,
        out_shape=(
            jax.ShapeDtypeStruct((1, ROWS, COLS), BF16),
            jax.ShapeDtypeStruct((ROWS, COLS), BF16),
            jax.ShapeDtypeStruct((COLS, RANK), F32),
        ),
        in_specs=[anywhere] * 3,
        out_specs=(anywhere,) * 3,
        scratch_shapes=scratch,
        compiler_params=pltpu.CompilerParams(
            collective_id=0, has_side_effects=True, vmem_limit_bytes=60 * 2**20
        ),
        cost_estimate=pl.CostEstimate(
            flops=12 * ROWS * COLS * RANK, bytes_accessed=6 * 2**20, transcendentals=0
        ),
    )(momentum, gradient, right_factor)


def solution(mesh):
    placed = (P("dp", "fsdp", "tensor"), P("dp", "fsdp", "tensor"), P("tensor", None))
    return jax.shard_map(
        shards,
        mesh=mesh,
        in_specs=placed,
        out_specs=(P("dp", "fsdp", "tensor"), P("fsdp", "tensor"), P("tensor", None)),
        check_vma=False,
    )
```

```python
import math

import jax
import jax.numpy as jnp
from jax import lax
from jax.experimental import pallas as pl
from jax.experimental.pallas import tpu as pltpu
from jax.sharding import PartitionSpec as P

D = 8192
FF = 14336
RANK = 128
MESH = pl.DeviceIdType.MESH
F32 = jnp.float32
BF16 = jnp.bfloat16
HIGHEST = lax.Precision.HIGHEST

NZ = 16
ROWS = 512
HALF = 256
COLS = 896
XCH = 32
WCH = 64
GCH = 8
TILES = COLS // 128
PLACES = COLS // WCH
NB = 16

NEAR_Z = [4, 3, -3, 2, -2, 1, -1]
FAR_Z = sorted(range(1, NZ), key=lambda d: -min(d, NZ - d))
NEAR_XY = [(1, 1), (1, 3), (0, 2), (1, 0), (3, 0), (0, 1), (0, 3), (0, 0)]
FAR_XY = sorted(
    [(dx, dy) for dx in range(4) for dy in range(4) if (dx, dy) != (0, 0)],
    key=lambda o: -(min(o[0], 4 - o[0]) + min(o[1], 4 - o[1])),
)


def split3(a):
    high = a.astype(BF16)
    rest = a - high.astype(F32)
    mid = rest.astype(BF16)
    low = (rest - mid.astype(F32)).astype(BF16)
    return high, mid, low


def outer_f32(u, v):
    u1, u2, u3 = split3(u)
    v1, v2, v3 = split3(v)
    left = jnp.concatenate([u1, u1, u2, u1, u2, u3], 0)
    right = jnp.concatenate([v1, v2, v1, v3, v2, v1], 0)
    return lax.dot_general(left, right, (((0,), (0,)), ((), ())), preferred_element_type=F32)


def inverse_cholesky(a_ref, e_ref, panels):
    if panels[0] == 0:
        rows = lax.broadcasted_iota(jnp.int32, (RANK, RANK), 0)
        cols = lax.broadcasted_iota(jnp.int32, (RANK, RANK), 1)
        e_ref[...] = jnp.where(rows == cols, 1.0, 0.0).astype(F32)
    sub = lax.broadcasted_iota(jnp.int32, (NB, RANK), 0)

    def spread(t, j):
        return jnp.broadcast_to(t[j : j + 1, :], (NB, RANK))

    for base in [p * NB for p in panels]:
        xa = a_ref[base : base + NB, :]
        xe = e_ref[base : base + NB, :]
        col = [
            jnp.broadcast_to(xa[:, base + k : base + k + 1], (NB, RANK)) for k in range(NB)
        ]
        va, ve, out = [], [], []
        for j in range(NB):
            pivot = spread(col[j], j)
            inv = 1.0 / pivot
            row_e = spread(xe, j)
            out.append((row_e * lax.rsqrt(pivot))[0:1])
            row_a = inv * spread(xa, j)
            row_e = inv * row_e
            va.append(row_a[0:1])
            ve.append(row_e[0:1])
            if j + 1 < NB:
                below = jnp.where(sub > j, col[j], 0.0)
                xa = xa - below * row_a
                xe = xe - below * row_e
                for k in range(j + 1, NB):
                    col[k] = col[k] - below * (inv * spread(col[k], j))
        last = base + NB
        if last < RANK:
            v = jnp.concatenate([jnp.concatenate(va, 0), jnp.concatenate(ve, 0)], 1)
            change = outer_f32(xa, v)
            a_ref[last:, :] = a_ref[last:, :] - change[last:, :RANK]
            e_ref[last:, :] = e_ref[last:, :] - change[last:, RANK:]
        e_ref[base:last, :] = jnp.concatenate(out, 0)


def right_times(tiles_ref, m):
    parts = jnp.concatenate(split3(m), 0)
    out = []
    for i in range(TILES):
        tile = tiles_ref[i * 128 : (i + 1) * 128, :]
        r = lax.dot_general(tile, parts, (((0,), (1,)), ((), ())), preferred_element_type=F32)
        out.append(r[:, :RANK] + (r[:, RANK : 2 * RANK] + r[:, 2 * RANK :]))
    return out


def rows_times(x, m):
    r = lax.dot_general(
        x, jnp.concatenate(split3(m), 0), (((1,), (1,)), ((), ())), preferred_element_type=F32
    )
    return r[:, :RANK] + (r[:, RANK : 2 * RANK] + r[:, 2 * RANK :])


def kernel(
    mom, grad, fac, new_mom, update, new_fac,
    m_v, g_v, f_v, fb, own, oth, xs0, xr0, xs1, xr1, xo, xp, xl, xoth, ws, wr, wo, wp, wa, gs, gr, go, gp,
    qs, qr, lower, a_s, right, ob, acc, load, send, recv,
):
    c = lax.axis_index("dp")
    f = lax.axis_index("fsdp")
    t = lax.axis_index("tensor")
    x = f // 4
    y = lax.rem(f, 4)
    other = 1 - c
    partner = (other, f, t)

    def core(dc):
        return c if dc == 0 else other

    def along_z(d, dc=0):
        return (core(dc), f, lax.rem(t + d + NZ, NZ))

    def along_xy(dx, dy, dc=0):
        return (core(dc), lax.rem(x + dx, 4) * 4 + lax.rem(y + dy, 4), t)

    def pair_of(chip):
        px = chip // 4
        return lax.rem(px, 2) * 4 + lax.rem(lax.rem(chip, 4) + 2 * (px // 2), 4)

    pair = pair_of(f)
    half = x // 2
    place = c * 8 + pair
    owner = place < PLACES
    idle = jnp.logical_not(owner)
    ring = [along_z(d) for d in FAR_Z]
    chips = [along_xy(*o) for o in FAR_XY]
    near = [(2 * (len(NEAR_XY) - 1 - i) + dc, along_xy(*o, dc)) for i, o in enumerate(NEAR_XY) for dc in (0, 1)]
    near = [(slot, to) for slot, to in near if slot]

    def chunk(index, size):
        return pl.ds(pl.multiple_of(index * size, size), size)

    def put(src, dst, phase, to):
        pltpu.make_async_remote_copy(
            src_ref=src, dst_ref=dst, send_sem=send.at[phase], recv_sem=recv.at[phase],
            device_id=to, device_id_type=MESH,
        ).start()

    def got(region, phase):
        pltpu.make_async_remote_copy(
            src_ref=region, dst_ref=region, send_sem=send.at[phase], recv_sem=recv.at[phase],
            device_id=partner, device_id_type=MESH,
        ).wait_recv()

    def sent(region, phase):
        pltpu.make_async_remote_copy(
            src_ref=region, dst_ref=region, send_sem=send.at[phase], recv_sem=recv.at[phase],
            device_id=partner, device_id_type=MESH,
        ).wait_send()

    def summed(ref, it, size, count):
        total = ref[it, 0:size, :].astype(F32)
        for k in range(1, count):
            total = total + ref[it, k * size : (k + 1) * size, :].astype(F32)
        return total

    greet = ring + [along_z(d, 1) for d in (4, -4, 3, -3, 2, -2, 1, -1)] + [partner]
    for o in FAR_XY:
        greet += [along_xy(*o), along_xy(*o, 1)]
    barrier = pltpu.get_barrier_semaphore()
    for to in greet:
        pl.semaphore_signal(barrier, inc=1, device_id=to, device_id_type=MESH)

    load_f = pltpu.make_async_copy(fac, f_v, load.at[8])
    load_f.start()
    loads = []
    for i in range(4):
        r = pl.ds(i * 128, 128)
        pair_in = [
            pltpu.make_async_copy(mom.at[0, r], m_v.at[r], load.at[2 * i]),
            pltpu.make_async_copy(grad.at[0, r], g_v.at[r], load.at[2 * i + 1]),
        ]
        for copy in pair_in:
            copy.start()
        loads.append(pair_in)
    load_f.wait()
    fb[...] = f_v[...].astype(BF16)
    for i in range(4):
        for copy in loads[i]:
            copy.wait()
        r = pl.ds(i * 128, 128)
        block = (m_v[r, :].astype(F32) + g_v[r, :].astype(F32)).astype(BF16)
        own[r, :] = block
        xs0[r, :] = (0.5 * jnp.dot(block, fb[...], preferred_element_type=F32)).astype(BF16)

    mine = pl.ds(pl.multiple_of(c * HALF, HALF), HALF)
    theirs = pl.ds(pl.multiple_of(other * HALF, HALF), HALF)
    nt = (((1,), (1,)), ((), ()))
    tn = (((0,), (0,)), ((), ()))

    def phase(it, k):
        return 2 + 8 * it + k

    def left_spread(it, total):
        xo[it] = total.astype(BF16)
        for to in ring:
            put(xo.at[it], xp.at[it, chunk(t, XCH)], phase(it, 1), to)
        xp[it, chunk(t, XCH), :] = total.astype(BF16)

    def left_here(it):
        got(xp.at[it, pl.ds(0, (NZ - 1) * XCH)], phase(it, 1))
        both = xp[it, 0:HALF, :].astype(F32) + xp[it, HALF : 2 * HALF, :].astype(F32)
        return both.astype(BF16)

    def right_out(it, left):
        part = lax.dot_general(left, own[mine, :], tn, preferred_element_type=F32)
        part = part + lax.dot_general(left, oth[...], tn, preferred_element_type=F32)
        part = (0.5 * part).astype(BF16)
        for i in range(TILES):
            ws[it, i * 128 : (i + 1) * 128, :] = part[:, i * 128 : (i + 1) * 128]
        for slot, to in near:
            there = to[0] * 8 + pair_of(to[1])

            @pl.when(there < PLACES)
            def _():
                put(ws.at[it, chunk(there, WCH)], wr.at[it, pl.ds(slot * WCH, WCH)], phase(it, 2), to)

        @pl.when(owner)
        def _():
            wr[it, 0:WCH, :] = ws[it, chunk(place, WCH), :]

    def right_spread(it):
        @pl.when(owner)
        def _():
            got(wr.at[it, pl.ds(WCH, 15 * WCH)], phase(it, 2))
            total = summed(wr, it, WCH, 16).astype(BF16)
            wo[it] = total
            rows = chunk(half * 8 + pair, WCH)
            for to in chips:
                put(wo.at[it], wp.at[it, rows], phase(it, 3), to)
            wp[it, rows, :] = total

    def right_join(it):
        @pl.when(c == 0)
        def _():
            got(wp.at[it, pl.ds(0, 15 * WCH)], phase(it, 3))
            both = wp[it, 0:512, :].astype(F32) + wp[it, 512:1024, :].astype(F32)
            wa[it, 0:512, :] = both.astype(BF16)
            put(wa.at[it, pl.ds(0, 512)], wa.at[it, pl.ds(0, 512)], phase(it, 4), partner)

        @pl.when(c == 1)
        def _():
            @pl.when(owner)
            def _():
                got(wp.at[it, pl.ds(0, 11 * WCH)], phase(it, 3))

            @pl.when(idle)
            def _():
                got(wp.at[it, pl.ds(0, 12 * WCH)], phase(it, 3))

            both = wp[it, 0:384, :].astype(F32) + wp[it, 512:896, :].astype(F32)
            wa[it, 512:896, :] = both.astype(BF16)
            put(wa.at[it, pl.ds(512, 384)], wa.at[it, pl.ds(512, 384)], phase(it, 4), partner)

    def right_here(it):
        @pl.when(c == 0)
        def _():
            got(wa.at[it, pl.ds(512, 384)], phase(it, 4))

        @pl.when(c == 1)
        def _():
            got(wa.at[it, pl.ds(0, 512)], phase(it, 4))

    def gram_out(it, left):
        gs[it] = lax.dot_general(left, left, tn, preferred_element_type=F32)
        for slot, to in near:
            there = to[0] * 8 + pair_of(to[1])
            put(gs.at[it, chunk(there, GCH)], gr.at[it, pl.ds(slot * GCH, GCH)], phase(it, 5), to)
        gr[it, 0:GCH, :] = gs[it, chunk(place, GCH), :]

    def gram_spread(it):
        got(gr.at[it, pl.ds(GCH, 15 * GCH)], phase(it, 5))
        total = summed(gr, it, GCH, 16)
        go[it] = total
        rows = chunk(half * 16 + place, GCH)
        for o in FAR_XY:
            for dc in (0, 1):
                put(go.at[it], gp.at[it, rows], phase(it, 6), along_xy(*o, dc))
        put(go.at[it], gp.at[it, rows], phase(it, 6), partner)
        gp[it, rows, :] = total

    def gram_here(it):
        got(gp.at[it, pl.ds(0, 31 * GCH)], phase(it, 6))
        return gp[it, 0:RANK, :] + gp[it, RANK : 2 * RANK, :]

    def squares_out(it, tiles):
        total = jnp.sum(tiles[0] * tiles[0], axis=0, keepdims=True)
        for tile in tiles[1:]:
            total = total + jnp.sum(tile * tile, axis=0, keepdims=True)
        qs[it] = jnp.broadcast_to(total, (8, RANK))
        for to in ring:
            put(qs.at[it], qr.at[it, chunk(t, 8)], phase(it, 7), to)
        qr[it, chunk(t, 8), :] = qs[it]

    def norms(it):
        got(qr.at[it, pl.ds(0, (NZ - 1) * 8)], phase(it, 7))
        return jnp.sqrt(summed(qr, it, 8, NZ)[0:1, :] + 1e-06)

    pl.semaphore_wait(barrier, len(greet))
    for d in NEAR_Z + [0]:
        for dc in (0, 1):
            if (d, dc) == (0, 0):
                continue
            to = along_z(d, dc)
            src = xs0.at[chunk(to[0] * 8 + lax.rem(to[2], 8), XCH)]
            put(src, xr0.at[0, pl.ds((2 * (d % 8) + dc) * XCH, XCH)], phase(0, 0), to)
    xr0[0, 0:XCH, :] = xs0[chunk(c * 8 + lax.rem(t, 8), XCH), :]
    put(own.at[theirs], oth, 0, partner)
    got(xr0.at[0, pl.ds(XCH, 15 * XCH)], phase(0, 0))
    left_spread(0, summed(xr0, 0, XCH, 16))
    got(oth, 0)
    left = left_here(0)
    right_out(0, left)
    gram_out(0, left)
    right_spread(0)
    gram_spread(0)
    right_join(0)

    def products(first, last):
        tiles = [wa[0, i * 128 : (i + 1) * 128, :] for i in range(first, last)]
        tiles = jnp.concatenate(tiles, 1)
        cols = pl.ds(first * 128, (last - first) * 128)
        part = lax.dot_general(own[mine, cols], tiles, nt, preferred_element_type=F32)
        return part + lax.dot_general(oth[:, cols], tiles, nt, preferred_element_type=F32)

    @pl.when(c == 0)
    def _():
        acc[...] = products(0, 4)

    @pl.when(c == 1)
    def _():
        acc[...] = products(4, 7)

    right_here(0)

    @pl.when(c == 0)
    def _():
        xs1[0] = (0.5 * (acc[...] + products(4, 7))).astype(BF16)

    @pl.when(c == 1)
    def _():
        xs1[0] = (0.5 * (acc[...] + products(0, 4))).astype(BF16)

    for d in NEAR_Z:
        to = along_z(d)
        src = xs1.at[0, chunk(lax.rem(to[2], 8), XCH)]
        put(src, xr1.at[0, pl.ds((d % 8) * XCH, XCH)], phase(1, 0), to)
    xr1[0, 0:XCH, :] = xs1[0, chunk(lax.rem(t, 8), XCH), :]
    a_s[...] = gram_here(0)
    inverse_cholesky(a_s, lower.at[0], range(8))
    got(xr1.at[0, pl.ds(XCH, 7 * XCH)], phase(1, 0))
    owned = summed(xr1, 0, XCH, 8)
    left_spread(
        1,
        lax.dot_general(owned, lower[0], nt, preferred_element_type=F32, precision=HIGHEST),
    )
    squares_out(0, right_times(wa.at[0], lower[0]))
    left = left_here(1)
    gram_out(1, left)
    right_out(1, left)
    xl[...] = left
    put(xl, xoth, 1, partner)
    gram_spread(1)
    right_spread(1)
    scale = jnp.broadcast_to(1.0 / norms(0), (RANK, RANK))
    a_s[...] = gram_here(1) * scale * scale.T
    inverse_cholesky(a_s, lower.at[1], range(4))
    right_join(1)
    inverse_cholesky(a_s, lower.at[1], range(4, 8))
    mix = lower[1] * scale
    right_here(1)
    tiles = right_times(wa.at[1], mix)
    squares_out(1, tiles)
    for i in range(TILES):
        right[i * 128 : (i + 1) * 128, :] = tiles[i]
    got(xoth, 1)
    ob[mine, :] = rows_times(xl[...], mix).astype(BF16)
    ob[theirs, :] = rows_times(xoth[...], mix).astype(BF16)
    right_b = right[...].astype(BF16)
    for i in range(4):
        r = pl.ds(i * 128, 128)
        feedback = lax.dot_general(ob[r, :], right_b, nt, preferred_element_type=F32)
        new_mom[0, r, :] = (own[r, :].astype(F32) - 0.05 * feedback).astype(BF16)

    sent(oth, 0)
    sent(xl, 1)
    sent(xr0.at[0, pl.ds(0, 15 * XCH)], phase(0, 0))
    sent(xr1.at[0, pl.ds(0, 7 * XCH)], phase(1, 0))
    for it in range(2):
        sent(xp.at[it, pl.ds(0, (NZ - 1) * XCH)], phase(it, 1))

        @pl.when(owner)
        def _():
            sent(wr.at[it, pl.ds(0, 13 * WCH)], phase(it, 2))
            sent(wr.at[it, pl.ds(0, 15 * WCH)], phase(it, 3))

        @pl.when(idle)
        def _():
            sent(wr.at[it, pl.ds(0, 14 * WCH)], phase(it, 2))

        @pl.when(c == 0)
        def _():
            sent(wa.at[it, pl.ds(0, 512)], phase(it, 4))

        @pl.when(c == 1)
        def _():
            sent(wa.at[it, pl.ds(512, 384)], phase(it, 4))

        sent(gr.at[it, pl.ds(0, 15 * GCH)], phase(it, 5))
        sent(gp.at[it, pl.ds(0, 31 * GCH)], phase(it, 6))
        sent(qr.at[it, pl.ds(0, (NZ - 1) * 8)], phase(it, 7))

    new_fac[...] = right[...] * (1.0 / norms(1))
    factor_b = new_fac[...].astype(BF16)
    for i in range(4):
        r = pl.ds(i * 128, 128)
        low_rank = lax.dot_general(ob[r, :], factor_b, nt, preferred_element_type=F32)
        update[r, :] = (math.sqrt(D * FF / RANK) * low_rank).astype(BF16)


def shards(momentum, gradient, right_factor):
    scratch = [
        pltpu.VMEM((ROWS, COLS), BF16),
        pltpu.VMEM((ROWS, COLS), BF16),
        pltpu.VMEM((COLS, RANK), F32),
        pltpu.VMEM((COLS, RANK), BF16),
        pltpu.VMEM((ROWS, COLS), BF16),
        pltpu.VMEM((HALF, COLS), BF16),
        pltpu.VMEM((ROWS, RANK), BF16),
        pltpu.VMEM((1, 16 * XCH, RANK), BF16),
        pltpu.VMEM((1, HALF, RANK), BF16),
        pltpu.VMEM((1, 8 * XCH, RANK), BF16),
        pltpu.VMEM((2, XCH, RANK), BF16),
        pltpu.VMEM((2, NZ * XCH, RANK), BF16),
        pltpu.VMEM((HALF, RANK), BF16),
        pltpu.VMEM((HALF, RANK), BF16),
        pltpu.VMEM((2, COLS, RANK), BF16),
        pltpu.VMEM((2, 16 * WCH, RANK), BF16),
        pltpu.VMEM((2, WCH, RANK), BF16),
        pltpu.VMEM((2, 16 * WCH, RANK), BF16),
        pltpu.VMEM((2, COLS, RANK), BF16),
        pltpu.VMEM((2, RANK, RANK), F32),
        pltpu.VMEM((2, 16 * GCH, RANK), F32),
        pltpu.VMEM((2, GCH, RANK), F32),
        pltpu.VMEM((2, 32 * GCH, RANK), F32),
        pltpu.VMEM((2, 8, RANK), F32),
        pltpu.VMEM((2, NZ * 8, RANK), F32),
        pltpu.VMEM((2, RANK, RANK), F32),
        pltpu.VMEM((RANK, RANK), F32),
        pltpu.VMEM((COLS, RANK), F32),
        pltpu.VMEM((ROWS, RANK), BF16),
        pltpu.VMEM((HALF, RANK), F32),
        pltpu.SemaphoreType.DMA((9,)),
        pltpu.SemaphoreType.DMA((18,)),
        pltpu.SemaphoreType.DMA((18,)),
    ]
    arguments = [
        pltpu.with_memory_space_constraint(v, pltpu.HBM)
        for v in (momentum, gradient, right_factor)
    ]
    return pl.pallas_call(
        kernel,
        out_shape=(
            jax.ShapeDtypeStruct((1, ROWS, COLS), BF16),
            jax.ShapeDtypeStruct((ROWS, COLS), BF16),
            jax.ShapeDtypeStruct((COLS, RANK), F32),
        ),
        in_specs=[pl.BlockSpec(memory_space=pl.ANY)] * 3,
        out_specs=(pl.BlockSpec(memory_space=pltpu.VMEM),) * 3,
        scratch_shapes=scratch,
        compiler_params=pltpu.CompilerParams(
            collective_id=0, has_side_effects=True, vmem_limit_bytes=40 * 2**20
        ),
        cost_estimate=pl.CostEstimate(
            flops=12 * ROWS * COLS * RANK, bytes_accessed=6 * 2**20, transcendentals=0
        ),
    )(*arguments)


def solution(mesh):
    placed = (P("dp", "fsdp", "tensor"), P("dp", "fsdp", "tensor"), P("tensor", None))
    return jax.shard_map(
        shards,
        mesh=mesh,
        in_specs=placed,
        out_specs=(P("dp", "fsdp", "tensor"), P("fsdp", "tensor"), P("tensor", None)),
        check_vma=False,
    )
```

```python
import math

import jax
import jax.numpy as jnp
from jax import lax
from jax.experimental import pallas as pl
from jax.experimental.pallas import tpu as pltpu
from jax.sharding import PartitionSpec as P

D = 8192
FF = 14336
RANK = 128
MESH = pl.DeviceIdType.MESH
F32 = jnp.float32
BF16 = jnp.bfloat16

NZ = 16
ROWS = 512
HALF = 256
COLS = 896
XCH = 32
WCH = 64
GCH = 8
TILES = COLS // 128
PLACES = COLS // WCH
NB = 16

NEAR_Z = [4, 3, -3, 2, -2, 1, -1]
FAR_Z = sorted(range(1, NZ), key=lambda d: -min(d, NZ - d))
NEAR_XY = [(1, 1), (1, 3), (0, 2), (1, 0), (3, 0), (0, 1), (0, 3), (0, 0)]
FAR_XY = sorted(
    [(dx, dy) for dx in range(4) for dy in range(4) if (dx, dy) != (0, 0)],
    key=lambda o: -(min(o[0], 4 - o[0]) + min(o[1], 4 - o[1])),
)


def split3(a):
    high = a.astype(BF16)
    rest = a - high.astype(F32)
    mid = rest.astype(BF16)
    low = (rest - mid.astype(F32)).astype(BF16)
    return high, mid, low


def outer_f32(u, v):
    u1, u2, u3 = split3(u)
    v1, v2, v3 = split3(v)
    left = jnp.concatenate([u1, u1, u2, u1, u2, u3], 0)
    right = jnp.concatenate([v1, v2, v1, v3, v2, v1], 0)
    return lax.dot_general(left, right, (((0,), (0,)), ((), ())), preferred_element_type=F32)


def inverse_cholesky(a_ref, e_ref, panels):
    if panels[0] == 0:
        rows = lax.broadcasted_iota(jnp.int32, (RANK, RANK), 0)
        cols = lax.broadcasted_iota(jnp.int32, (RANK, RANK), 1)
        e_ref[...] = jnp.where(rows == cols, 1.0, 0.0).astype(F32)
    sub = lax.broadcasted_iota(jnp.int32, (NB, RANK), 0)

    def spread(t, j):
        return jnp.broadcast_to(t[j : j + 1, :], (NB, RANK))

    for base in [p * NB for p in panels]:
        xa = a_ref[base : base + NB, :]
        xe = e_ref[base : base + NB, :]
        col = [
            jnp.broadcast_to(xa[:, base + k : base + k + 1], (NB, RANK)) for k in range(NB)
        ]
        va, ve, out = [], [], []
        for j in range(NB):
            pivot = spread(col[j], j)
            inv = 1.0 / pivot
            row_e = spread(xe, j)
            out.append((row_e * lax.rsqrt(pivot))[0:1])
            row_a = inv * spread(xa, j)
            row_e = inv * row_e
            va.append(row_a[0:1])
            ve.append(row_e[0:1])
            if j + 1 < NB:
                below = jnp.where(sub > j, col[j], 0.0)
                xa = xa - below * row_a
                xe = xe - below * row_e
                for k in range(j + 1, NB):
                    col[k] = col[k] - below * (inv * spread(col[k], j))
        last = base + NB
        if last < RANK:
            v = jnp.concatenate([jnp.concatenate(va, 0), jnp.concatenate(ve, 0)], 1)
            change = outer_f32(xa, v)
            a_ref[last:, :] = a_ref[last:, :] - change[last:, :RANK]
            e_ref[last:, :] = e_ref[last:, :] - change[last:, RANK:]
        e_ref[base:last, :] = jnp.concatenate(out, 0)


def right_times(tiles_ref, m):
    parts = jnp.concatenate(split3(m)[:2], 0)
    out = []
    for i in range(TILES):
        tile = tiles_ref[i * 128 : (i + 1) * 128, :]
        r = lax.dot_general(tile, parts, (((0,), (1,)), ((), ())), preferred_element_type=F32)
        out.append(r[:, :RANK] + r[:, RANK:])
    return out


def rows_times(x, m):
    parts = jnp.concatenate(split3(m)[:2], 0)
    r = lax.dot_general(x, parts, (((1,), (1,)), ((), ())), preferred_element_type=F32)
    return r[:, :RANK] + r[:, RANK:]


def kernel(
    mom, grad, fac, new_mom, right, ob, norm,
    m_v, g_v, f_v, fb, own, oth, xs0, xr0, xs1, xr1, xo, xp, xl, xoth, ws, wr, wo, wp, wa, gs, gr, go, gp, ga,
    qs, qr, lower, a_s, acc, load, send, recv,
):
    c = lax.axis_index("dp")
    f = lax.axis_index("fsdp")
    t = lax.axis_index("tensor")
    x = f // 4
    y = lax.rem(f, 4)
    other = 1 - c
    partner = (other, f, t)

    def core(dc):
        return c if dc == 0 else other

    def along_z(d, dc=0):
        return (core(dc), f, lax.rem(t + d + NZ, NZ))

    def along_xy(dx, dy, dc=0):
        return (core(dc), lax.rem(x + dx, 4) * 4 + lax.rem(y + dy, 4), t)

    def pair_of(chip):
        px = chip // 4
        return lax.rem(px, 2) * 4 + lax.rem(lax.rem(chip, 4) + 2 * (px // 2), 4)

    pair = pair_of(f)
    half = x // 2
    place = c * 8 + pair
    owner = place < PLACES
    idle = jnp.logical_not(owner)
    ring = [along_z(d) for d in FAR_Z]
    chips = [along_xy(*o) for o in FAR_XY]
    near = [(2 * (len(NEAR_XY) - 1 - i) + dc, along_xy(*o, dc)) for i, o in enumerate(NEAR_XY) for dc in (0, 1)]
    near = [(slot, to) for slot, to in near if slot]

    def chunk(index, size):
        return pl.ds(pl.multiple_of(index * size, size), size)

    def put(src, dst, phase, to):
        pltpu.make_async_remote_copy(
            src_ref=src, dst_ref=dst, send_sem=send.at[phase], recv_sem=recv.at[phase],
            device_id=to, device_id_type=MESH,
        ).start()

    def got(region, phase):
        pltpu.make_async_remote_copy(
            src_ref=region, dst_ref=region, send_sem=send.at[phase], recv_sem=recv.at[phase],
            device_id=partner, device_id_type=MESH,
        ).wait_recv()

    def sent(region, phase):
        pltpu.make_async_remote_copy(
            src_ref=region, dst_ref=region, send_sem=send.at[phase], recv_sem=recv.at[phase],
            device_id=partner, device_id_type=MESH,
        ).wait_send()

    def summed(ref, it, size, count):
        total = ref[it, 0:size, :].astype(F32)
        for k in range(1, count):
            total = total + ref[it, k * size : (k + 1) * size, :].astype(F32)
        return total

    greet = [along_z(d, dc) for d in (4, -4, 3, -3, 2, -2, 1, -1) for dc in (0, 1)] + [partner]
    for o in FAR_XY:
        greet += [along_xy(*o), along_xy(*o, 1)]
    barrier = pltpu.get_barrier_semaphore()
    for to in greet:
        pl.semaphore_signal(barrier, inc=1, device_id=to, device_id_type=MESH)

    load_f = pltpu.make_async_copy(fac, f_v, load.at[8])
    load_f.start()
    loads = []
    for i in range(4):
        r = pl.ds(i * 128, 128)
        pair_in = [
            pltpu.make_async_copy(mom.at[0, r], m_v.at[r], load.at[2 * i]),
            pltpu.make_async_copy(grad.at[0, r], g_v.at[r], load.at[2 * i + 1]),
        ]
        for copy in pair_in:
            copy.start()
        loads.append(pair_in)
    load_f.wait()
    fb[...] = f_v[...].astype(BF16)
    for i in range(4):
        for copy in loads[i]:
            copy.wait()
        r = pl.ds(i * 128, 128)
        block = (m_v[r, :].astype(F32) + g_v[r, :].astype(F32)).astype(BF16)
        own[r, :] = block
        xs0[r, :] = (0.5 * jnp.dot(block, fb[...], preferred_element_type=F32)).astype(BF16)

    mine = pl.ds(pl.multiple_of(c * HALF, HALF), HALF)
    theirs = pl.ds(pl.multiple_of(other * HALF, HALF), HALF)
    nt = (((1,), (1,)), ((), ()))
    tn = (((0,), (0,)), ((), ()))

    def phase(it, k):
        return 2 + 9 * it + k

    def left_spread(it, total):
        xo[it] = total.astype(BF16)
        for to in ring:
            put(xo.at[it], xp.at[it, chunk(t, XCH)], phase(it, 1), to)
        xp[it, chunk(t, XCH), :] = total.astype(BF16)

    def left_here(it):
        got(xp.at[it, pl.ds(0, (NZ - 1) * XCH)], phase(it, 1))
        both = xp[it, 0:HALF, :].astype(F32) + xp[it, HALF : 2 * HALF, :].astype(F32)
        return both.astype(BF16)

    def right_out(it, left):
        part = lax.dot_general(left, own[mine, :], tn, preferred_element_type=F32)
        part = part + lax.dot_general(left, oth[...], tn, preferred_element_type=F32)
        part = (0.5 * part).astype(BF16)
        for i in range(TILES):
            ws[it, i * 128 : (i + 1) * 128, :] = part[:, i * 128 : (i + 1) * 128]
        for slot, to in near:
            there = to[0] * 8 + pair_of(to[1])

            @pl.when(there < PLACES)
            def _():
                put(ws.at[it, chunk(there, WCH)], wr.at[it, pl.ds(slot * WCH, WCH)], phase(it, 2), to)

        @pl.when(owner)
        def _():
            wr[it, 0:WCH, :] = ws[it, chunk(place, WCH), :]

    def right_spread(it):
        @pl.when(owner)
        def _():
            got(wr.at[it, pl.ds(WCH, 15 * WCH)], phase(it, 2))
            total = summed(wr, it, WCH, 16).astype(BF16)
            wo[it] = total
            rows = chunk(half * 8 + pair, WCH)
            for to in chips:
                put(wo.at[it], wp.at[it, rows], phase(it, 3), to)
            wp[it, rows, :] = total

    def right_join(it):
        @pl.when(c == 0)
        def _():
            got(wp.at[it, pl.ds(0, 15 * WCH)], phase(it, 3))
            both = wp[it, 0:512, :].astype(F32) + wp[it, 512:1024, :].astype(F32)
            wa[it, 0:512, :] = both.astype(BF16)
            put(wa.at[it, pl.ds(0, 512)], wa.at[it, pl.ds(0, 512)], phase(it, 4), partner)

        @pl.when(c == 1)
        def _():
            @pl.when(owner)
            def _():
                got(wp.at[it, pl.ds(0, 11 * WCH)], phase(it, 3))

            @pl.when(idle)
            def _():
                got(wp.at[it, pl.ds(0, 12 * WCH)], phase(it, 3))

            both = wp[it, 0:384, :].astype(F32) + wp[it, 512:896, :].astype(F32)
            wa[it, 512:896, :] = both.astype(BF16)
            put(wa.at[it, pl.ds(512, 384)], wa.at[it, pl.ds(512, 384)], phase(it, 4), partner)

    def right_here(it):
        @pl.when(c == 0)
        def _():
            got(wa.at[it, pl.ds(512, 384)], phase(it, 4))

        @pl.when(c == 1)
        def _():
            got(wa.at[it, pl.ds(0, 512)], phase(it, 4))

    def gram_out(it, left):
        gs[it] = lax.dot_general(left, left, tn, preferred_element_type=F32)
        for slot, to in near:
            there = to[0] * 8 + pair_of(to[1])
            put(gs.at[it, chunk(there, GCH)], gr.at[it, pl.ds(slot * GCH, GCH)], phase(it, 5), to)
        gr[it, 0:GCH, :] = gs[it, chunk(place, GCH), :]

    def gram_spread(it):
        got(gr.at[it, pl.ds(GCH, 15 * GCH)], phase(it, 5))
        total = summed(gr, it, GCH, 16)
        go[it] = total
        rows = chunk(half * 8 + pair, GCH)
        for to in chips:
            put(go.at[it], gp.at[it, rows], phase(it, 6), to)
        gp[it, rows, :] = total

    def gram_join(it):
        got(gp.at[it, pl.ds(0, 15 * GCH)], phase(it, 6))
        rows = chunk(c, RANK // 2)
        ga[it, rows, :] = gp[it, 0 : RANK // 2, :] + gp[it, RANK // 2 : RANK, :]
        put(ga.at[it, rows], ga.at[it, rows], phase(it, 8), partner)

    def gram_here(it):
        got(ga.at[it, pl.ds(0, RANK // 2)], phase(it, 8))
        return ga[it]

    def squares_out(it, tiles):
        total = jnp.sum(tiles[0] * tiles[0], axis=0, keepdims=True)
        for tile in tiles[1:]:
            total = total + jnp.sum(tile * tile, axis=0, keepdims=True)
        qs[it] = jnp.broadcast_to(total, (8, RANK))
        for to in ring:
            put(qs.at[it], qr.at[it, chunk(t, 8)], phase(it, 7), to)
        qr[it, chunk(t, 8), :] = qs[it]

    def norms(it):
        got(qr.at[it, pl.ds(0, (NZ - 1) * 8)], phase(it, 7))
        return jnp.sqrt(summed(qr, it, 8, NZ)[0:1, :] + 1e-06)

    pl.semaphore_wait(barrier, len(greet))
    for d in NEAR_Z + [0]:
        for dc in (0, 1):
            if (d, dc) == (0, 0):
                continue
            to = along_z(d, dc)
            src = xs0.at[chunk(to[0] * 8 + lax.rem(to[2], 8), XCH)]
            put(src, xr0.at[0, pl.ds((2 * (d % 8) + dc) * XCH, XCH)], phase(0, 0), to)
    xr0[0, 0:XCH, :] = xs0[chunk(c * 8 + lax.rem(t, 8), XCH), :]
    put(own.at[theirs], oth, 0, partner)
    got(xr0.at[0, pl.ds(XCH, 15 * XCH)], phase(0, 0))
    left_spread(0, summed(xr0, 0, XCH, 16))
    got(oth, 0)
    left = left_here(0)
    right_out(0, left)
    gram_out(0, left)
    right_spread(0)
    gram_spread(0)
    right_join(0)

    def products(first, last):
        tiles = [wa[0, i * 128 : (i + 1) * 128, :] for i in range(first, last)]
        tiles = jnp.concatenate(tiles, 1)
        cols = pl.ds(first * 128, (last - first) * 128)
        part = lax.dot_general(own[mine, cols], tiles, nt, preferred_element_type=F32)
        return part + lax.dot_general(oth[:, cols], tiles, nt, preferred_element_type=F32)

    @pl.when(c == 0)
    def _():
        acc[...] = products(0, 4)

    @pl.when(c == 1)
    def _():
        acc[...] = products(4, 7)

    right_here(0)

    @pl.when(c == 0)
    def _():
        xs1[0] = (0.5 * (acc[...] + products(4, 7))).astype(BF16)

    @pl.when(c == 1)
    def _():
        xs1[0] = (0.5 * (acc[...] + products(0, 4))).astype(BF16)

    for d in NEAR_Z:
        to = along_z(d)
        src = xs1.at[0, chunk(lax.rem(to[2], 8), XCH)]
        put(src, xr1.at[0, pl.ds((d % 8) * XCH, XCH)], phase(1, 0), to)
    xr1[0, 0:XCH, :] = xs1[0, chunk(lax.rem(t, 8), XCH), :]
    gram_join(0)
    a_s[...] = gram_here(0)
    inverse_cholesky(a_s, lower.at[0], range(8))
    low_parts = split3(lower[0])
    low_parts = jnp.concatenate([low_parts[0], low_parts[1], low_parts[0]], 1)
    got(xr1.at[0, pl.ds(XCH, 7 * XCH)], phase(1, 0))
    owned = split3(summed(xr1, 0, XCH, 8))
    owned = jnp.concatenate([owned[0], owned[0], owned[1]], 1)
    left_spread(1, lax.dot_general(owned, low_parts, nt, preferred_element_type=F32))
    squares_out(0, right_times(wa.at[0], lower[0]))
    left = left_here(1)
    gram_out(1, left)
    right_out(1, left)
    xl[...] = left
    put(xl, xoth, 1, partner)
    gram_spread(1)
    right_spread(1)
    scale = jnp.broadcast_to(1.0 / norms(0), (RANK, RANK))
    gram_join(1)
    a_s[...] = gram_here(1) * scale * scale.T
    inverse_cholesky(a_s, lower.at[1], range(4))
    right_join(1)
    inverse_cholesky(a_s, lower.at[1], range(4, 8))
    mix = lower[1] * scale
    right_here(1)
    tiles = right_times(wa.at[1], mix)
    squares_out(1, tiles)
    for i in range(TILES):
        right[i * 128 : (i + 1) * 128, :] = tiles[i]
    got(xoth, 1)
    ob[mine, :] = rows_times(xl[...], mix).astype(BF16)
    ob[theirs, :] = rows_times(xoth[...], mix).astype(BF16)
    right_b = right[...].astype(BF16)
    for i in range(4):
        r = pl.ds(i * 128, 128)
        feedback = lax.dot_general(ob[r, :], right_b, nt, preferred_element_type=F32)
        new_mom[0, r, :] = (own[r, :].astype(F32) - 0.05 * feedback).astype(BF16)

    sent(oth, 0)
    sent(xl, 1)
    sent(xr0.at[0, pl.ds(0, 15 * XCH)], phase(0, 0))
    sent(xr1.at[0, pl.ds(0, 7 * XCH)], phase(1, 0))
    for it in range(2):
        sent(xp.at[it, pl.ds(0, (NZ - 1) * XCH)], phase(it, 1))

        @pl.when(owner)
        def _():
            sent(wr.at[it, pl.ds(0, 13 * WCH)], phase(it, 2))
            sent(wr.at[it, pl.ds(0, 15 * WCH)], phase(it, 3))

        @pl.when(idle)
        def _():
            sent(wr.at[it, pl.ds(0, 14 * WCH)], phase(it, 2))

        @pl.when(c == 0)
        def _():
            sent(wa.at[it, pl.ds(0, 512)], phase(it, 4))

        @pl.when(c == 1)
        def _():
            sent(wa.at[it, pl.ds(512, 384)], phase(it, 4))

        sent(gr.at[it, pl.ds(0, 15 * GCH)], phase(it, 5))
        sent(gp.at[it, pl.ds(0, 15 * GCH)], phase(it, 6))
        sent(ga.at[it, pl.ds(0, RANK // 2)], phase(it, 8))
        sent(qr.at[it, pl.ds(0, (NZ - 1) * 8)], phase(it, 7))

    norm[...] = jnp.broadcast_to(1.0 / norms(1), (8, RANK))


def finish(new_mom, right, ob, norm, new_mom_out, update, new_fac, fac, up, sem):
    first = pltpu.make_async_copy(new_mom, new_mom_out, sem.at[0])
    first.start()
    fac[...] = right[...] * norm[0:1, :]
    copies = [first, pltpu.make_async_copy(fac, new_fac, sem.at[1])]
    copies[1].start()
    factor_b = fac[...].astype(BF16)
    nt = (((1,), (1,)), ((), ()))
    for i in range(4):
        r = pl.ds(i * 128, 128)
        low_rank = lax.dot_general(ob[r, :], factor_b, nt, preferred_element_type=F32)
        up[r, :] = (math.sqrt(D * FF / RANK) * low_rank).astype(BF16)
        copy = pltpu.make_async_copy(up.at[r], update.at[r], sem.at[2 + i])
        copy.start()
        copies.append(copy)
    for copy in copies:
        copy.wait()


def shards(momentum, gradient, right_factor):
    scratch = [
        pltpu.VMEM((ROWS, COLS), BF16),
        pltpu.VMEM((ROWS, COLS), BF16),
        pltpu.VMEM((COLS, RANK), F32),
        pltpu.VMEM((COLS, RANK), BF16),
        pltpu.VMEM((ROWS, COLS), BF16),
        pltpu.VMEM((HALF, COLS), BF16),
        pltpu.VMEM((ROWS, RANK), BF16),
        pltpu.VMEM((1, 16 * XCH, RANK), BF16),
        pltpu.VMEM((1, HALF, RANK), BF16),
        pltpu.VMEM((1, 8 * XCH, RANK), BF16),
        pltpu.VMEM((2, XCH, RANK), BF16),
        pltpu.VMEM((2, NZ * XCH, RANK), BF16),
        pltpu.VMEM((HALF, RANK), BF16),
        pltpu.VMEM((HALF, RANK), BF16),
        pltpu.VMEM((2, COLS, RANK), BF16),
        pltpu.VMEM((2, 16 * WCH, RANK), BF16),
        pltpu.VMEM((2, WCH, RANK), BF16),
        pltpu.VMEM((2, 16 * WCH, RANK), BF16),
        pltpu.VMEM((2, COLS, RANK), BF16),
        pltpu.VMEM((2, RANK, RANK), F32),
        pltpu.VMEM((2, 16 * GCH, RANK), F32),
        pltpu.VMEM((2, GCH, RANK), F32),
        pltpu.VMEM((2, 16 * GCH, RANK), F32),
        pltpu.VMEM((2, RANK, RANK), F32),
        pltpu.VMEM((2, 8, RANK), F32),
        pltpu.VMEM((2, NZ * 8, RANK), F32),
        pltpu.VMEM((2, RANK, RANK), F32),
        pltpu.VMEM((RANK, RANK), F32),
        pltpu.VMEM((HALF, RANK), F32),
        pltpu.SemaphoreType.DMA((9,)),
        pltpu.SemaphoreType.DMA((20,)),
        pltpu.SemaphoreType.DMA((20,)),
    ]
    arguments = [
        pltpu.with_memory_space_constraint(v, pltpu.HBM)
        for v in (momentum, gradient, right_factor)
    ]
    vmem = pl.BlockSpec(memory_space=pltpu.VMEM)
    anywhere = pl.BlockSpec(memory_space=pl.ANY)
    made = pl.pallas_call(
        kernel,
        out_shape=(
            jax.ShapeDtypeStruct((1, ROWS, COLS), BF16),
            jax.ShapeDtypeStruct((COLS, RANK), F32),
            jax.ShapeDtypeStruct((ROWS, RANK), BF16),
            jax.ShapeDtypeStruct((8, RANK), F32),
        ),
        in_specs=[anywhere] * 3,
        out_specs=(vmem,) * 4,
        scratch_shapes=scratch,
        compiler_params=pltpu.CompilerParams(
            collective_id=0, has_side_effects=True, vmem_limit_bytes=40 * 2**20
        ),
        cost_estimate=pl.CostEstimate(
            flops=10 * ROWS * COLS * RANK, bytes_accessed=4 * 2**20, transcendentals=0
        ),
    )(*arguments)
    return pl.pallas_call(
        finish,
        out_shape=(
            jax.ShapeDtypeStruct((1, ROWS, COLS), BF16),
            jax.ShapeDtypeStruct((ROWS, COLS), BF16),
            jax.ShapeDtypeStruct((COLS, RANK), F32),
        ),
        in_specs=[vmem] * 4,
        out_specs=(anywhere,) * 3,
        scratch_shapes=[
            pltpu.VMEM((COLS, RANK), F32),
            pltpu.VMEM((ROWS, COLS), BF16),
            pltpu.SemaphoreType.DMA((6,)),
        ],
        compiler_params=pltpu.CompilerParams(vmem_limit_bytes=40 * 2**20),
        cost_estimate=pl.CostEstimate(
            flops=2 * ROWS * COLS * RANK, bytes_accessed=3 * 2**20, transcendentals=0
        ),
    )(*made)


def solution(mesh):
    placed = (P("dp", "fsdp", "tensor"), P("dp", "fsdp", "tensor"), P("tensor", None))
    return jax.shard_map(
        shards,
        mesh=mesh,
        in_specs=placed,
        out_specs=(P("dp", "fsdp", "tensor"), P("fsdp", "tensor"), P("tensor", None)),
        check_vma=False,
    )
```

```python
import math

import jax
import jax.numpy as jnp
from jax import lax
from jax.experimental import pallas as pl
from jax.experimental.pallas import tpu as pltpu
from jax.sharding import PartitionSpec as P

D = 8192
FF = 14336
RANK = 128
MESH = pl.DeviceIdType.MESH
F32 = jnp.float32
BF16 = jnp.bfloat16

NZ = 16
ROWS = 512
HALF = 256
COLS = 896
XCH = 32
WCH = 64
GCH = 8
TILES = COLS // 128
PLACES = COLS // WCH
NB = 16

NEAR_Z = [4, 3, -3, 2, -2, 1, -1]
FAR_Z = sorted(range(1, NZ), key=lambda d: -min(d, NZ - d))
NEAR_XY = [(1, 1), (1, 3), (0, 2), (1, 0), (3, 0), (0, 1), (0, 3), (0, 0)]
FAR_XY = sorted(
    [(dx, dy) for dx in range(4) for dy in range(4) if (dx, dy) != (0, 0)],
    key=lambda o: -(min(o[0], 4 - o[0]) + min(o[1], 4 - o[1])),
)


def split3(a):
    high = a.astype(BF16)
    rest = a - high.astype(F32)
    mid = rest.astype(BF16)
    low = (rest - mid.astype(F32)).astype(BF16)
    return high, mid, low


def outer_f32(u, v):
    u1, u2, u3 = split3(u)
    v1, v2, v3 = split3(v)
    left = jnp.concatenate([u1, u1, u2, u1, u2, u3], 0)
    right = jnp.concatenate([v1, v2, v1, v3, v2, v1], 0)
    return lax.dot_general(left, right, (((0,), (0,)), ((), ())), preferred_element_type=F32)


def inverse_cholesky(a_ref, e_ref, panels):
    if panels[0] == 0:
        rows = lax.broadcasted_iota(jnp.int32, (RANK, RANK), 0)
        cols = lax.broadcasted_iota(jnp.int32, (RANK, RANK), 1)
        e_ref[...] = jnp.where(rows == cols, 1.0, 0.0).astype(F32)
    sub = lax.broadcasted_iota(jnp.int32, (NB, RANK), 0)

    def spread(t, j):
        return jnp.broadcast_to(t[j : j + 1, :], (NB, RANK))

    for base in [p * NB for p in panels]:
        xa = a_ref[base : base + NB, :]
        xe = e_ref[base : base + NB, :]
        col = [
            jnp.broadcast_to(xa[:, base + k : base + k + 1], (NB, RANK)) for k in range(NB)
        ]
        va, ve, out = [], [], []
        for j in range(NB):
            pivot = spread(col[j], j)
            inv = 1.0 / pivot
            row_e = spread(xe, j)
            out.append((row_e * lax.rsqrt(pivot))[0:1])
            row_a = inv * spread(xa, j)
            row_e = inv * row_e
            va.append(row_a[0:1])
            ve.append(row_e[0:1])
            if j + 1 < NB:
                below = jnp.where(sub > j, col[j], 0.0)
                xa = xa - below * row_a
                xe = xe - below * row_e
                for k in range(j + 1, NB):
                    col[k] = col[k] - below * (inv * spread(col[k], j))
        last = base + NB
        if last < RANK:
            v = jnp.concatenate([jnp.concatenate(va, 0), jnp.concatenate(ve, 0)], 1)
            change = outer_f32(xa, v)
            a_ref[last:, :] = a_ref[last:, :] - change[last:, :RANK]
            e_ref[last:, :] = e_ref[last:, :] - change[last:, RANK:]
        e_ref[base:last, :] = jnp.concatenate(out, 0)


def right_times(tiles_ref, m):
    parts = jnp.concatenate(split3(m)[:2], 0)
    out = []
    for i in range(TILES):
        tile = tiles_ref[i * 128 : (i + 1) * 128, :]
        r = lax.dot_general(tile, parts, (((0,), (1,)), ((), ())), preferred_element_type=F32)
        out.append(r[:, :RANK] + r[:, RANK:])
    return out


def rows_times(x, m):
    parts = jnp.concatenate(split3(m)[:2], 0)
    r = lax.dot_general(x, parts, (((1,), (1,)), ((), ())), preferred_element_type=F32)
    return r[:, :RANK] + r[:, RANK:]


def kernel(
    mom, grad, fac, new_mom, right, ob, norm,
    m_v, g_v, f_v, fb, own, oth, xs0, xr0, xs1, xr1, xo, xp, xl, xoth, ws, wr, wo, wp, wa, gs, gr, go, gp0, gp1, ga,
    qs, qr, lower, a_s, acc, load, send, recv,
):
    c = lax.axis_index("dp")
    f = lax.axis_index("fsdp")
    t = lax.axis_index("tensor")
    x = f // 4
    y = lax.rem(f, 4)
    other = 1 - c
    partner = (other, f, t)

    def core(dc):
        return c if dc == 0 else other

    def along_z(d, dc=0):
        return (core(dc), f, lax.rem(t + d + NZ, NZ))

    def along_xy(dx, dy, dc=0):
        return (core(dc), lax.rem(x + dx, 4) * 4 + lax.rem(y + dy, 4), t)

    def pair_of(chip):
        px = chip // 4
        return lax.rem(px, 2) * 4 + lax.rem(lax.rem(chip, 4) + 2 * (px // 2), 4)

    pair = pair_of(f)
    half = x // 2
    place = c * 8 + pair
    owner = place < PLACES
    idle = jnp.logical_not(owner)
    ring = [along_z(d) for d in FAR_Z]
    chips = [along_xy(*o) for o in FAR_XY]
    near = [(2 * (len(NEAR_XY) - 1 - i) + dc, along_xy(*o, dc)) for i, o in enumerate(NEAR_XY) for dc in (0, 1)]
    near = [(slot, to) for slot, to in near if slot]

    def chunk(index, size):
        return pl.ds(pl.multiple_of(index * size, size), size)

    def put(src, dst, phase, to):
        pltpu.make_async_remote_copy(
            src_ref=src, dst_ref=dst, send_sem=send.at[phase], recv_sem=recv.at[phase],
            device_id=to, device_id_type=MESH,
        ).start()

    def got(region, phase):
        pltpu.make_async_remote_copy(
            src_ref=region, dst_ref=region, send_sem=send.at[phase], recv_sem=recv.at[phase],
            device_id=partner, device_id_type=MESH,
        ).wait_recv()

    def sent(region, phase):
        pltpu.make_async_remote_copy(
            src_ref=region, dst_ref=region, send_sem=send.at[phase], recv_sem=recv.at[phase],
            device_id=partner, device_id_type=MESH,
        ).wait_send()

    def summed(ref, it, size, count):
        total = ref[it, 0:size, :].astype(F32)
        for k in range(1, count):
            total = total + ref[it, k * size : (k + 1) * size, :].astype(F32)
        return total

    greet = [along_z(d, dc) for d in (4, -4) for dc in (0, 1)]
    greet += [along_xy(*o, dc) for o in FAR_XY[:5] for dc in (0, 1)]
    greet += [along_z(d, dc) for d in (3, -3, 2, -2, 1, -1) for dc in (0, 1)]
    greet += [along_xy(*o, dc) for o in FAR_XY[5:] for dc in (0, 1)] + [partner]
    barrier = pltpu.get_barrier_semaphore()

    def signal(some):
        for to in some:
            pl.semaphore_signal(barrier, inc=1, device_id=to, device_id_type=MESH)

    signal(greet[:14])
    load_f = pltpu.make_async_copy(fac, f_v, load.at[8])
    load_f.start()
    loads = []
    for i in range(4):
        r = pl.ds(i * 128, 128)
        pair_in = [
            pltpu.make_async_copy(mom.at[0, r], m_v.at[r], load.at[2 * i]),
            pltpu.make_async_copy(grad.at[0, r], g_v.at[r], load.at[2 * i + 1]),
        ]
        for copy in pair_in:
            copy.start()
        loads.append(pair_in)
    signal(greet[14:])
    load_f.wait()
    fb[...] = f_v[...].astype(BF16)
    for i in range(4):
        for copy in loads[i]:
            copy.wait()
        r = pl.ds(i * 128, 128)
        block = (m_v[r, :].astype(F32) + g_v[r, :].astype(F32)).astype(BF16)
        own[r, :] = block
        xs0[r, :] = (0.5 * jnp.dot(block, fb[...], preferred_element_type=F32)).astype(BF16)

    mine = pl.ds(pl.multiple_of(c * HALF, HALF), HALF)
    theirs = pl.ds(pl.multiple_of(other * HALF, HALF), HALF)
    nt = (((1,), (1,)), ((), ()))
    tn = (((0,), (0,)), ((), ()))

    def phase(it, k):
        return 2 + 9 * it + k

    def left_spread(it, total):
        xo[it] = total.astype(BF16)
        for to in ring:
            put(xo.at[it], xp.at[it, chunk(t, XCH)], phase(it, 1), to)
        xp[it, chunk(t, XCH), :] = total.astype(BF16)

    def left_here(it):
        got(xp.at[it, pl.ds(0, (NZ - 1) * XCH)], phase(it, 1))
        both = xp[it, 0:HALF, :].astype(F32) + xp[it, HALF : 2 * HALF, :].astype(F32)
        return both.astype(BF16)

    def right_out(it, left):
        part = lax.dot_general(left, own[mine, :], tn, preferred_element_type=F32)
        part = part + lax.dot_general(left, oth[...], tn, preferred_element_type=F32)
        part = (0.5 * part).astype(BF16)
        for i in range(TILES):
            ws[it, i * 128 : (i + 1) * 128, :] = part[:, i * 128 : (i + 1) * 128]
        for slot, to in near:
            there = to[0] * 8 + pair_of(to[1])

            @pl.when(there < PLACES)
            def _():
                put(ws.at[it, chunk(there, WCH)], wr.at[it, pl.ds(slot * WCH, WCH)], phase(it, 2), to)

        @pl.when(owner)
        def _():
            wr[it, 0:WCH, :] = ws[it, chunk(place, WCH), :]

    def right_spread(it):
        @pl.when(owner)
        def _():
            got(wr.at[it, pl.ds(WCH, 15 * WCH)], phase(it, 2))
            total = summed(wr, it, WCH, 16).astype(BF16)
            wo[it] = total
            rows = chunk(half * 8 + pair, WCH)
            for to in chips:
                put(wo.at[it], wp.at[it, rows], phase(it, 3), to)
            wp[it, rows, :] = total

    def right_join(it):
        @pl.when(c == 0)
        def _():
            got(wp.at[it, pl.ds(0, 15 * WCH)], phase(it, 3))
            both = wp[it, 0:512, :].astype(F32) + wp[it, 512:1024, :].astype(F32)
            wa[it, 0:512, :] = both.astype(BF16)
            put(wa.at[it, pl.ds(0, 512)], wa.at[it, pl.ds(0, 512)], phase(it, 4), partner)

        @pl.when(c == 1)
        def _():
            @pl.when(owner)
            def _():
                got(wp.at[it, pl.ds(0, 11 * WCH)], phase(it, 3))

            @pl.when(idle)
            def _():
                got(wp.at[it, pl.ds(0, 12 * WCH)], phase(it, 3))

            both = wp[it, 0:384, :].astype(F32) + wp[it, 512:896, :].astype(F32)
            wa[it, 512:896, :] = both.astype(BF16)
            put(wa.at[it, pl.ds(512, 384)], wa.at[it, pl.ds(512, 384)], phase(it, 4), partner)

    def right_here(it):
        @pl.when(c == 0)
        def _():
            got(wa.at[it, pl.ds(512, 384)], phase(it, 4))

        @pl.when(c == 1)
        def _():
            got(wa.at[it, pl.ds(0, 512)], phase(it, 4))

    def gram_out(it, left):
        gs[it] = lax.dot_general(left, left, tn, preferred_element_type=F32)
        for slot, to in near:
            there = to[0] * 8 + pair_of(to[1])
            put(gs.at[it, chunk(there, GCH)], gr.at[it, pl.ds(slot * GCH, GCH)], phase(it, 5), to)
        gr[it, 0:GCH, :] = gs[it, chunk(place, GCH), :]

    def gram_owned(it):
        got(gr.at[it, pl.ds(GCH, 15 * GCH)], phase(it, 5))
        total = summed(gr, it, GCH, 16)
        go[it] = total
        return total

    def gram_spread_core(total):
        rows = chunk(half * 8 + pair, GCH)
        for to in chips:
            put(go.at[0], gp0.at[0, rows], phase(0, 6), to)
        gp0[0, rows, :] = total

    def gram_join_core():
        got(gp0.at[0, pl.ds(0, 15 * GCH)], phase(0, 6))
        rows = chunk(c, RANK // 2)
        ga[rows, :] = gp0[0, 0 : RANK // 2, :] + gp0[0, RANK // 2 : RANK, :]
        put(ga.at[rows], ga.at[rows], phase(0, 8), partner)
        got(ga.at[pl.ds(0, RANK // 2)], phase(0, 8))
        return ga[...]

    def gram_spread_all(total):
        rows = chunk(half * 16 + place, GCH)
        for o in FAR_XY:
            for dc in (0, 1):
                put(go.at[1], gp1.at[0, rows], phase(1, 6), along_xy(*o, dc))
        put(go.at[1], gp1.at[0, rows], phase(1, 6), partner)
        gp1[0, rows, :] = total

    def gram_join_all():
        got(gp1.at[0, pl.ds(0, 31 * GCH)], phase(1, 6))
        return gp1[0, 0:RANK, :] + gp1[0, RANK : 2 * RANK, :]

    def squares_sum(it, tiles):
        total = jnp.sum(tiles[0] * tiles[0], axis=0, keepdims=True)
        for tile in tiles[1:]:
            total = total + jnp.sum(tile * tile, axis=0, keepdims=True)
        qs[it] = jnp.broadcast_to(total, (8, RANK))

    def squares_send(it):
        for to in ring:
            put(qs.at[it], qr.at[it, chunk(t, 8)], phase(it, 7), to)
        qr[it, chunk(t, 8), :] = qs[it]

    def norms(it):
        got(qr.at[it, pl.ds(0, (NZ - 1) * 8)], phase(it, 7))
        return jnp.sqrt(summed(qr, it, 8, NZ)[0:1, :] + 1e-06)

    pl.semaphore_wait(barrier, len(greet))
    for d in NEAR_Z + [0]:
        for dc in (0, 1):
            if (d, dc) == (0, 0):
                continue
            to = along_z(d, dc)
            src = xs0.at[chunk(to[0] * 8 + lax.rem(to[2], 8), XCH)]
            put(src, xr0.at[0, pl.ds((2 * (d % 8) + dc) * XCH, XCH)], phase(0, 0), to)
    xr0[0, 0:XCH, :] = xs0[chunk(c * 8 + lax.rem(t, 8), XCH), :]
    put(own.at[theirs], oth, 0, partner)
    got(xr0.at[0, pl.ds(XCH, 15 * XCH)], phase(0, 0))
    left_spread(0, summed(xr0, 0, XCH, 16))
    got(oth, 0)
    left = left_here(0)
    right_out(0, left)
    gram_out(0, left)
    right_spread(0)
    gram_spread_core(gram_owned(0))
    right_join(0)

    def products(first, last):
        tiles = [wa[0, i * 128 : (i + 1) * 128, :] for i in range(first, last)]
        tiles = jnp.concatenate(tiles, 1)
        cols = pl.ds(first * 128, (last - first) * 128)
        part = lax.dot_general(own[mine, cols], tiles, nt, preferred_element_type=F32)
        return part + lax.dot_general(oth[:, cols], tiles, nt, preferred_element_type=F32)

    @pl.when(c == 0)
    def _():
        acc[...] = products(0, 4)

    @pl.when(c == 1)
    def _():
        acc[...] = products(4, 7)

    right_here(0)

    @pl.when(c == 0)
    def _():
        xs1[0] = (0.5 * (acc[...] + products(4, 7))).astype(BF16)

    @pl.when(c == 1)
    def _():
        xs1[0] = (0.5 * (acc[...] + products(0, 4))).astype(BF16)

    for d in NEAR_Z:
        to = along_z(d)
        src = xs1.at[0, chunk(lax.rem(to[2], 8), XCH)]
        put(src, xr1.at[0, pl.ds((d % 8) * XCH, XCH)], phase(1, 0), to)
    xr1[0, 0:XCH, :] = xs1[0, chunk(lax.rem(t, 8), XCH), :]
    a_s[...] = gram_join_core()
    inverse_cholesky(a_s, lower.at[0], range(8))
    low_parts = split3(lower[0])
    low_parts = jnp.concatenate([low_parts[0], low_parts[1], low_parts[0]], 1)
    got(xr1.at[0, pl.ds(XCH, 7 * XCH)], phase(1, 0))
    owned = split3(summed(xr1, 0, XCH, 8))
    owned = jnp.concatenate([owned[0], owned[0], owned[1]], 1)
    left_spread(1, lax.dot_general(owned, low_parts, nt, preferred_element_type=F32))
    squares_sum(0, right_times(wa.at[0], lower[0]))
    left = left_here(1)
    gram_out(1, left)
    right_out(1, left)
    xl[...] = left
    put(xl, xoth, 1, partner)
    squares_send(0)
    gram_spread_all(gram_owned(1))
    right_spread(1)
    scale = jnp.broadcast_to(1.0 / norms(0), (RANK, RANK))
    a_s[...] = gram_join_all() * scale * scale.T
    inverse_cholesky(a_s, lower.at[1], range(4))
    right_join(1)
    inverse_cholesky(a_s, lower.at[1], range(4, 8))
    mix = lower[1] * scale
    right_here(1)
    tiles = right_times(wa.at[1], mix)
    squares_sum(1, tiles)
    squares_send(1)
    for i in range(TILES):
        right[i * 128 : (i + 1) * 128, :] = tiles[i]
    got(xoth, 1)
    ob[mine, :] = rows_times(xl[...], mix).astype(BF16)
    ob[theirs, :] = rows_times(xoth[...], mix).astype(BF16)
    right_b = right[...].astype(BF16)
    for i in range(4):
        r = pl.ds(i * 128, 128)
        feedback = lax.dot_general(ob[r, :], right_b, nt, preferred_element_type=F32)
        new_mom[0, r, :] = (own[r, :].astype(F32) - 0.05 * feedback).astype(BF16)

    sent(oth, 0)
    sent(xl, 1)
    sent(xr0.at[0, pl.ds(0, 15 * XCH)], phase(0, 0))
    sent(xr1.at[0, pl.ds(0, 7 * XCH)], phase(1, 0))
    sent(gp0.at[0, pl.ds(0, 15 * GCH)], phase(0, 6))
    sent(ga.at[pl.ds(0, RANK // 2)], phase(0, 8))
    sent(gp1.at[0, pl.ds(0, 31 * GCH)], phase(1, 6))
    for it in range(2):
        sent(xp.at[it, pl.ds(0, (NZ - 1) * XCH)], phase(it, 1))

        @pl.when(owner)
        def _():
            sent(wr.at[it, pl.ds(0, 13 * WCH)], phase(it, 2))
            sent(wr.at[it, pl.ds(0, 15 * WCH)], phase(it, 3))

        @pl.when(idle)
        def _():
            sent(wr.at[it, pl.ds(0, 14 * WCH)], phase(it, 2))

        @pl.when(c == 0)
        def _():
            sent(wa.at[it, pl.ds(0, 512)], phase(it, 4))

        @pl.when(c == 1)
        def _():
            sent(wa.at[it, pl.ds(512, 384)], phase(it, 4))

        sent(gr.at[it, pl.ds(0, 15 * GCH)], phase(it, 5))
        sent(qr.at[it, pl.ds(0, (NZ - 1) * 8)], phase(it, 7))

    norm[...] = jnp.broadcast_to(1.0 / norms(1), (8, RANK))


def finish(new_mom, right, ob, norm, new_mom_out, update, new_fac, fac, up, sem):
    first = pltpu.make_async_copy(new_mom, new_mom_out, sem.at[0])
    first.start()
    fac[...] = right[...] * norm[0:1, :]
    copies = [first, pltpu.make_async_copy(fac, new_fac, sem.at[1])]
    copies[1].start()
    factor_b = fac[...].astype(BF16)
    nt = (((1,), (1,)), ((), ()))
    for i in range(4):
        r = pl.ds(i * 128, 128)
        low_rank = lax.dot_general(ob[r, :], factor_b, nt, preferred_element_type=F32)
        up[r, :] = (math.sqrt(D * FF / RANK) * low_rank).astype(BF16)
        copy = pltpu.make_async_copy(up.at[r], update.at[r], sem.at[2 + i])
        copy.start()
        copies.append(copy)
    for copy in copies:
        copy.wait()


def shards(momentum, gradient, right_factor):
    scratch = [
        pltpu.VMEM((ROWS, COLS), BF16),
        pltpu.VMEM((ROWS, COLS), BF16),
        pltpu.VMEM((COLS, RANK), F32),
        pltpu.VMEM((COLS, RANK), BF16),
        pltpu.VMEM((ROWS, COLS), BF16),
        pltpu.VMEM((HALF, COLS), BF16),
        pltpu.VMEM((ROWS, RANK), BF16),
        pltpu.VMEM((1, 16 * XCH, RANK), BF16),
        pltpu.VMEM((1, HALF, RANK), BF16),
        pltpu.VMEM((1, 8 * XCH, RANK), BF16),
        pltpu.VMEM((2, XCH, RANK), BF16),
        pltpu.VMEM((2, NZ * XCH, RANK), BF16),
        pltpu.VMEM((HALF, RANK), BF16),
        pltpu.VMEM((HALF, RANK), BF16),
        pltpu.VMEM((2, COLS, RANK), BF16),
        pltpu.VMEM((2, 16 * WCH, RANK), BF16),
        pltpu.VMEM((2, WCH, RANK), BF16),
        pltpu.VMEM((2, 16 * WCH, RANK), BF16),
        pltpu.VMEM((2, COLS, RANK), BF16),
        pltpu.VMEM((2, RANK, RANK), F32),
        pltpu.VMEM((2, 16 * GCH, RANK), F32),
        pltpu.VMEM((2, GCH, RANK), F32),
        pltpu.VMEM((1, 16 * GCH, RANK), F32),
        pltpu.VMEM((1, 32 * GCH, RANK), F32),
        pltpu.VMEM((RANK, RANK), F32),
        pltpu.VMEM((2, 8, RANK), F32),
        pltpu.VMEM((2, NZ * 8, RANK), F32),
        pltpu.VMEM((2, RANK, RANK), F32),
        pltpu.VMEM((RANK, RANK), F32),
        pltpu.VMEM((HALF, RANK), F32),
        pltpu.SemaphoreType.DMA((9,)),
        pltpu.SemaphoreType.DMA((20,)),
        pltpu.SemaphoreType.DMA((20,)),
    ]
    arguments = [
        pltpu.with_memory_space_constraint(v, pltpu.HBM)
        for v in (momentum, gradient, right_factor)
    ]
    vmem = pl.BlockSpec(memory_space=pltpu.VMEM)
    anywhere = pl.BlockSpec(memory_space=pl.ANY)
    made = pl.pallas_call(
        kernel,
        out_shape=(
            jax.ShapeDtypeStruct((1, ROWS, COLS), BF16),
            jax.ShapeDtypeStruct((COLS, RANK), F32),
            jax.ShapeDtypeStruct((ROWS, RANK), BF16),
            jax.ShapeDtypeStruct((8, RANK), F32),
        ),
        in_specs=[anywhere] * 3,
        out_specs=(vmem,) * 4,
        scratch_shapes=scratch,
        compiler_params=pltpu.CompilerParams(
            collective_id=0, has_side_effects=True, vmem_limit_bytes=40 * 2**20
        ),
        cost_estimate=pl.CostEstimate(
            flops=10 * ROWS * COLS * RANK, bytes_accessed=4 * 2**20, transcendentals=0
        ),
    )(*arguments)
    return pl.pallas_call(
        finish,
        out_shape=(
            jax.ShapeDtypeStruct((1, ROWS, COLS), BF16),
            jax.ShapeDtypeStruct((ROWS, COLS), BF16),
            jax.ShapeDtypeStruct((COLS, RANK), F32),
        ),
        in_specs=[vmem] * 4,
        out_specs=(anywhere,) * 3,
        scratch_shapes=[
            pltpu.VMEM((COLS, RANK), F32),
            pltpu.VMEM((ROWS, COLS), BF16),
            pltpu.SemaphoreType.DMA((6,)),
        ],
        compiler_params=pltpu.CompilerParams(vmem_limit_bytes=40 * 2**20),
        cost_estimate=pl.CostEstimate(
            flops=2 * ROWS * COLS * RANK, bytes_accessed=3 * 2**20, transcendentals=0
        ),
    )(*made)


def solution(mesh):
    placed = (P("dp", "fsdp", "tensor"), P("dp", "fsdp", "tensor"), P("tensor", None))
    return jax.shard_map(
        shards,
        mesh=mesh,
        in_specs=placed,
        out_specs=(P("dp", "fsdp", "tensor"), P("fsdp", "tensor"), P("tensor", None)),
        check_vma=False,
    )
```

```python
import math

import jax
import jax.numpy as jnp
from jax import lax
from jax.experimental import pallas as pl
from jax.experimental.pallas import tpu as pltpu
from jax.sharding import PartitionSpec as P

D = 8192
FF = 14336
RANK = 128
MESH = pl.DeviceIdType.MESH
F32 = jnp.float32
BF16 = jnp.bfloat16

NZ = 16
ROWS = 512
HALF = 256
COLS = 896
XCH = 32
WCH = 64
GCH = 8
TILES = COLS // 128
PLACES = COLS // WCH
NB = 16

NEAR_Z = [4, 3, -3, 2, -2, 1, -1]
FAR_Z = sorted(range(1, NZ), key=lambda d: -min(d, NZ - d))
NEAR_XY = [(1, 1), (1, 3), (0, 2), (1, 0), (3, 0), (0, 1), (0, 3), (0, 0)]
FAR_XY = sorted(
    [(dx, dy) for dx in range(4) for dy in range(4) if (dx, dy) != (0, 0)],
    key=lambda o: -(min(o[0], 4 - o[0]) + min(o[1], 4 - o[1])),
)


def split3(a):
    high = a.astype(BF16)
    rest = a - high.astype(F32)
    mid = rest.astype(BF16)
    low = (rest - mid.astype(F32)).astype(BF16)
    return high, mid, low


def inverse_cholesky(a_ref, e_ref, panels):
    if panels[0] == 0:
        rows = lax.broadcasted_iota(jnp.int32, (RANK, RANK), 0)
        cols = lax.broadcasted_iota(jnp.int32, (RANK, RANK), 1)
        e_ref[...] = jnp.where(rows == cols, 1.0, 0.0).astype(F32)
    sub = lax.broadcasted_iota(jnp.int32, (NB, RANK), 0)

    def spread(t, j):
        return jnp.broadcast_to(t[j : j + 1, :], (NB, RANK))

    for base in [p * NB for p in panels]:
        last = base + NB
        xa = a_ref[base:last, :]
        xe = e_ref[base:last, :]
        col = [
            jnp.broadcast_to(xa[:, base + k : base + k + 1], (NB, RANK)) for k in range(NB)
        ]
        if last < RANK:
            c1, c2, c3 = split3(a_ref[last:, base:last])
            below = jnp.concatenate([c1, c1, c2, c1, c2, c3], 1)
        inverses = jnp.zeros((NB, RANK), F32)
        out = jnp.zeros((NB, RANK), F32)
        for j in range(NB):
            inv = 1.0 / spread(col[j], j)
            inverses = jnp.where(sub == j, inv, inverses)
            row_e = spread(xe, j)
            out = jnp.where(sub == j, row_e, out)
            factor = jnp.where(sub != j, col[j] * inv, 0.0)
            xa = xa - factor * spread(xa, j)
            xe = xe - factor * row_e
            for k in range(j + 1, NB):
                col[k] = col[k] - factor * spread(col[k], j)
        e_ref[base:last, :] = out * jnp.sqrt(inverses)
        if last < RANK:
            v1, v2, v3 = split3(jnp.concatenate([xa * inverses, xe * inverses], 1))
            solved = jnp.concatenate([v1, v2, v1, v3, v2, v1], 0)
            change = jnp.dot(below, solved, preferred_element_type=F32)
            a_ref[last:, :] = a_ref[last:, :] - change[:, :RANK]
            e_ref[last:, :] = e_ref[last:, :] - change[:, RANK:]


def right_times(tiles_ref, m, first=0, last=TILES):
    parts = jnp.concatenate(split3(m)[:2], 0)
    out = []
    for i in range(first, last):
        tile = tiles_ref[i * 128 : (i + 1) * 128, :]
        r = lax.dot_general(tile, parts, (((0,), (1,)), ((), ())), preferred_element_type=F32)
        out.append(r[:, :RANK] + r[:, RANK:])
    return out


def rows_times(x, m):
    parts = jnp.concatenate(split3(m)[:2], 0)
    r = lax.dot_general(x, parts, (((1,), (1,)), ((), ())), preferred_element_type=F32)
    return r[:, :RANK] + r[:, RANK:]


def kernel(
    mom, grad, fac, new_mom, right, ob, norm,
    m_v, g_v, f_v, fb, own, oth, xs0, xr0, xs1, xr1, xo, xp, xl, xoth, ws, wr, wo, wp, wa, gs, gr, go, gp0, gp1, ga,
    qs, qr0, qr1, lower, a_s, acc, tally, load, send, recv,
):
    c = lax.axis_index("dp")
    f = lax.axis_index("fsdp")
    t = lax.axis_index("tensor")
    x = f // 4
    y = lax.rem(f, 4)
    other = 1 - c
    partner = (other, f, t)

    def core(dc):
        return c if dc == 0 else other

    def along_z(d, dc=0):
        return (core(dc), f, lax.rem(t + d + NZ, NZ))

    def near_z(d, dc=0):
        return along_z(4 + 8 * lax.rem(t, 2) if d == 4 else d, dc)

    def along_xy(dx, dy, dc=0):
        return (core(dc), lax.rem(x + dx, 4) * 4 + lax.rem(y + dy, 4), t)

    def pair_of(chip):
        px = chip // 4
        return lax.rem(px, 2) * 4 + lax.rem(lax.rem(chip, 4) + 2 * (px // 2), 4)

    pair = pair_of(f)
    half = x // 2
    place = c * 8 + pair
    owner = place < PLACES
    idle = jnp.logical_not(owner)
    ring = [along_z(d) for d in FAR_Z]
    chips = [along_xy(*o) for o in FAR_XY]
    near = [(2 * (len(NEAR_XY) - 1 - i) + dc, along_xy(*o, dc)) for i, o in enumerate(NEAR_XY) for dc in (0, 1)]
    near = [(slot, to) for slot, to in near if slot]

    def chunk(index, size):
        return pl.ds(pl.multiple_of(index * size, size), size)

    def put(src, dst, phase, to):
        pltpu.make_async_remote_copy(
            src_ref=src, dst_ref=dst, send_sem=send, recv_sem=recv.at[phase],
            device_id=to, device_id_type=MESH,
        ).start()

    def got(region, phase):
        pltpu.make_async_remote_copy(
            src_ref=region, dst_ref=region, send_sem=send, recv_sem=recv.at[phase],
            device_id=partner, device_id_type=MESH,
        ).wait_recv()

    def all_sent(rows):
        region = tally.at[pl.ds(0, rows)]
        pltpu.make_async_remote_copy(
            src_ref=region, dst_ref=region, send_sem=send, recv_sem=recv.at[0],
            device_id=partner, device_id_type=MESH,
        ).wait_send()

    def summed(ref, it, size, count):
        total = ref[it, 0:size, :].astype(F32)
        for k in range(1, count):
            total = total + ref[it, k * size : (k + 1) * size, :].astype(F32)
        return total

    greet = [along_z(d, dc) for d in (4, -4) for dc in (0, 1)]
    greet += [along_xy(*o, dc) for o in FAR_XY[:5] for dc in (0, 1)]
    greet += [along_z(d, dc) for d in (3, -3, 2, -2, 1, -1) for dc in (0, 1)]
    greet += [along_xy(*o, dc) for o in FAR_XY[5:] for dc in (0, 1)] + [partner]
    barrier = pltpu.get_barrier_semaphore()

    def signal(some):
        for to in some:
            pl.semaphore_signal(barrier, inc=1, device_id=to, device_id_type=MESH)

    signal(greet[:14])
    load_f = pltpu.make_async_copy(fac, f_v, load.at[4])
    load_f.start()
    for i in range(4):
        r = pl.ds(i * 128, 128)
        pair_in = [
            pltpu.make_async_copy(mom.at[0, r], m_v.at[r], load.at[i]),
            pltpu.make_async_copy(grad.at[0, r], g_v.at[r], load.at[i]),
        ]
        for copy in pair_in:
            copy.start()
    signal(greet[14:])
    load_f.wait()
    fb[...] = f_v[...].astype(BF16)
    for i in range(4):
        both = tally.at[pl.ds(0, 2 * 128 * TILES)]
        pltpu.make_async_copy(both, both, load.at[i]).wait()
        r = pl.ds(i * 128, 128)
        block = (m_v[r, :].astype(F32) + g_v[r, :].astype(F32)).astype(BF16)
        own[r, :] = block
        xs0[r, :] = (0.5 * jnp.dot(block, fb[...], preferred_element_type=F32)).astype(BF16)

    mine = pl.ds(pl.multiple_of(c * HALF, HALF), HALF)
    theirs = pl.ds(pl.multiple_of(other * HALF, HALF), HALF)
    nt = (((1,), (1,)), ((), ()))
    tn = (((0,), (0,)), ((), ()))

    def phase(it, k):
        return 2 + 9 * it + k

    def left_spread(it, total):
        xo[it] = total.astype(BF16)
        for to in ring:
            put(xo.at[it], xp.at[it, chunk(t, XCH)], phase(it, 1), to)
        xp[it, chunk(t, XCH), :] = total.astype(BF16)

    def left_here(it):
        got(xp.at[it, pl.ds(0, (NZ - 1) * XCH)], phase(it, 1))
        both = xp[it, 0:HALF, :].astype(F32) + xp[it, HALF : 2 * HALF, :].astype(F32)
        return both.astype(BF16)

    def right_out(it, left):
        part = lax.dot_general(left, own[mine, :], tn, preferred_element_type=F32)
        part = part + lax.dot_general(left, oth[...], tn, preferred_element_type=F32)
        part = (0.5 * part).astype(BF16)
        for i in range(TILES):
            ws[it, i * 128 : (i + 1) * 128, :] = part[:, i * 128 : (i + 1) * 128]
        for slot, to in near:
            there = to[0] * 8 + pair_of(to[1])

            @pl.when(there < PLACES)
            def _():
                put(ws.at[it, chunk(there, WCH)], wr.at[it, pl.ds(slot * WCH, WCH)], phase(it, 2), to)

        @pl.when(owner)
        def _():
            wr[it, 0:WCH, :] = ws[it, chunk(place, WCH), :]

    def right_spread(it):
        @pl.when(owner)
        def _():
            got(wr.at[it, pl.ds(WCH, 15 * WCH)], phase(it, 2))
            total = summed(wr, it, WCH, 16).astype(BF16)
            wo[it] = total
            rows = chunk(half * 8 + pair, WCH)
            for to in chips:
                put(wo.at[it], wp.at[it, rows], phase(it, 3), to)
            wp[it, rows, :] = total

    def right_join(it):
        @pl.when(c == 0)
        def _():
            got(wp.at[it, pl.ds(0, 15 * WCH)], phase(it, 3))
            both = wp[it, 0:512, :].astype(F32) + wp[it, 512:1024, :].astype(F32)
            wa[it, 0:512, :] = both.astype(BF16)
            put(wa.at[it, pl.ds(0, 512)], wa.at[it, pl.ds(0, 512)], phase(it, 4), partner)

        @pl.when(c == 1)
        def _():
            @pl.when(owner)
            def _():
                got(wp.at[it, pl.ds(0, 11 * WCH)], phase(it, 3))

            @pl.when(idle)
            def _():
                got(wp.at[it, pl.ds(0, 12 * WCH)], phase(it, 3))

            both = wp[it, 0:384, :].astype(F32) + wp[it, 512:896, :].astype(F32)
            wa[it, 512:896, :] = both.astype(BF16)
            put(wa.at[it, pl.ds(512, 384)], wa.at[it, pl.ds(512, 384)], phase(it, 4), partner)

    def right_here(it):
        @pl.when(c == 0)
        def _():
            got(wa.at[it, pl.ds(512, 384)], phase(it, 4))

        @pl.when(c == 1)
        def _():
            got(wa.at[it, pl.ds(0, 512)], phase(it, 4))

    def gram_out(it, left):
        gs[it] = lax.dot_general(left, left, tn, preferred_element_type=F32)
        for slot, to in near:
            there = to[0] * 8 + pair_of(to[1])
            put(gs.at[it, chunk(there, GCH)], gr.at[it, pl.ds(slot * GCH, GCH)], phase(it, 5), to)
        gr[it, 0:GCH, :] = gs[it, chunk(place, GCH), :]

    def gram_owned(it):
        got(gr.at[it, pl.ds(GCH, 15 * GCH)], phase(it, 5))
        total = summed(gr, it, GCH, 16)
        go[it] = total
        return total

    def gram_spread_core(total):
        rows = chunk(half * 8 + pair, GCH)
        for to in chips:
            put(go.at[0], gp0.at[0, rows], phase(0, 6), to)
        gp0[0, rows, :] = total

    def gram_join_core():
        got(gp0.at[0, pl.ds(0, 15 * GCH)], phase(0, 6))
        rows = chunk(c, RANK // 2)
        ga[rows, :] = gp0[0, 0 : RANK // 2, :] + gp0[0, RANK // 2 : RANK, :]
        put(ga.at[rows], ga.at[rows], phase(0, 8), partner)
        got(ga.at[pl.ds(0, RANK // 2)], phase(0, 8))
        return ga[...]

    def gram_spread_all(total):
        rows = chunk(half * 16 + place, GCH)
        for o in FAR_XY:
            for dc in (0, 1):
                put(go.at[1], gp1.at[0, rows], phase(1, 6), along_xy(*o, dc))
        put(go.at[1], gp1.at[0, rows], phase(1, 6), partner)
        gp1[0, rows, :] = total

    def gram_join_all():
        got(gp1.at[0, pl.ds(0, 31 * GCH)], phase(1, 6))
        return gp1[0, 0:RANK, :] + gp1[0, RANK : 2 * RANK, :]

    def squares_sum(it, tiles):
        total = jnp.sum(tiles[0] * tiles[0], axis=0, keepdims=True)
        for tile in tiles[1:]:
            total = total + jnp.sum(tile * tile, axis=0, keepdims=True)
        qs[it] = total

    def squares_send_core():
        for to in ring:
            put(qs.at[0], qr0.at[t], phase(0, 7), to)
        qr0[t] = qs[0]

    def squares_send_all():
        slot = 2 * t + c
        for d in FAR_Z:
            for dc in (0, 1):
                put(qs.at[1], qr1.at[slot], phase(1, 7), along_z(d, dc))
        put(qs.at[1], qr1.at[slot], phase(1, 7), partner)
        qr1[slot] = qs[1]

    def norms(it):
        ref, count = (qr0, NZ) if it == 0 else (qr1, 2 * NZ)
        got(ref.at[pl.ds(0, count - 1)], phase(it, 7))
        total = ref[0]
        for k in range(1, count):
            total = total + ref[k]
        return jnp.sqrt(total + 1e-06)

    pl.semaphore_wait(barrier, len(greet))
    for d in NEAR_Z + [0]:
        for dc in (0, 1):
            if (d, dc) == (0, 0):
                continue
            to = near_z(d, dc)
            src = xs0.at[chunk(to[0] * 8 + lax.rem(to[2], 8), XCH)]
            put(src, xr0.at[0, pl.ds((2 * (d % 8) + dc) * XCH, XCH)], phase(0, 0), to)
    xr0[0, 0:XCH, :] = xs0[chunk(c * 8 + lax.rem(t, 8), XCH), :]
    put(own.at[theirs], oth, 0, partner)
    got(xr0.at[0, pl.ds(XCH, 15 * XCH)], phase(0, 0))
    left_spread(0, summed(xr0, 0, XCH, 16))
    got(oth, 0)
    left = left_here(0)
    right_out(0, left)
    gram_out(0, left)
    right_spread(0)
    gram_spread_core(gram_owned(0))
    right_join(0)

    def products(first, last):
        tiles = [wa[0, i * 128 : (i + 1) * 128, :] for i in range(first, last)]
        tiles = jnp.concatenate(tiles, 1)
        cols = pl.ds(first * 128, (last - first) * 128)
        part = lax.dot_general(own[mine, cols], tiles, nt, preferred_element_type=F32)
        return part + lax.dot_general(oth[:, cols], tiles, nt, preferred_element_type=F32)

    @pl.when(c == 0)
    def _():
        acc[...] = products(0, 4)

    @pl.when(c == 1)
    def _():
        acc[...] = products(4, 7)

    right_here(0)

    @pl.when(c == 0)
    def _():
        xs1[0] = (0.5 * (acc[...] + products(4, 7))).astype(BF16)

    @pl.when(c == 1)
    def _():
        xs1[0] = (0.5 * (acc[...] + products(0, 4))).astype(BF16)

    for d in NEAR_Z:
        to = near_z(d)
        src = xs1.at[0, chunk(lax.rem(to[2], 8), XCH)]
        put(src, xr1.at[0, pl.ds((d % 8) * XCH, XCH)], phase(1, 0), to)
    xr1[0, 0:XCH, :] = xs1[0, chunk(lax.rem(t, 8), XCH), :]
    a_s[...] = gram_join_core()
    inverse_cholesky(a_s, lower.at[0], range(8))
    low_parts = split3(lower[0])
    low_parts = jnp.concatenate([low_parts[0], low_parts[1], low_parts[0]], 1)
    got(xr1.at[0, pl.ds(XCH, 7 * XCH)], phase(1, 0))
    owned = split3(summed(xr1, 0, XCH, 8))
    owned = jnp.concatenate([owned[0], owned[0], owned[1]], 1)
    left_spread(1, lax.dot_general(owned, low_parts, nt, preferred_element_type=F32))
    squares_sum(0, right_times(wa.at[0], lower[0]))
    left = left_here(1)
    gram_out(1, left)
    right_out(1, left)
    xl[...] = left
    put(xl, xoth, 1, partner)
    squares_send_core()
    gram_spread_all(gram_owned(1))
    right_spread(1)
    scale = jnp.broadcast_to(1.0 / norms(0), (RANK, RANK))
    a_s[...] = gram_join_all() * scale * scale.T
    inverse_cholesky(a_s, lower.at[1], range(8))
    mix = lower[1] * scale
    right_join(1)

    def right_tiles(first, last):
        tiles = right_times(wa.at[1], mix, first, last)
        for i in range(first, last):
            right[i * 128 : (i + 1) * 128, :] = tiles[i - first]
        return tiles

    @pl.when(c == 0)
    def _():
        squares_sum(1, right_tiles(0, 4))

    @pl.when(c == 1)
    def _():
        squares_sum(1, right_tiles(4, 7))

    squares_send_all()
    right_here(1)

    @pl.when(c == 0)
    def _():
        right_tiles(4, 7)

    @pl.when(c == 1)
    def _():
        right_tiles(0, 4)

    got(xoth, 1)
    ob[mine, :] = rows_times(xl[...], mix).astype(BF16)
    ob[theirs, :] = rows_times(xoth[...], mix).astype(BF16)
    right_b = right[...].astype(BF16)
    for i in range(4):
        r = pl.ds(i * 128, 128)
        feedback = lax.dot_general(ob[r, :], right_b, nt, preferred_element_type=F32)
        new_mom[0, r, :] = (own[r, :].astype(F32) - 0.05 * feedback).astype(BF16)

    everyone = 1792 + 256 + 480 + 224 + 2 * 480 + 2 * 240 + 240 + 496 + 128 + 30 + 62

    @pl.when(c == 0)
    def _():
        all_sent(everyone + 2 * (13 * WCH + 15 * WCH + 512))

    @pl.when((c == 1) & owner)
    def _():
        all_sent(everyone + 2 * (13 * WCH + 15 * WCH + 384))

    @pl.when(idle)
    def _():
        all_sent(everyone + 2 * (14 * WCH + 384))

    norm[...] = jnp.broadcast_to(1.0 / norms(1), (8, RANK))


def finish(new_mom, right, ob, norm, new_mom_out, update, new_fac, fac, up, sem):
    first = pltpu.make_async_copy(new_mom, new_mom_out, sem.at[0])
    first.start()
    fac[...] = right[...] * norm[0:1, :]
    copies = [first, pltpu.make_async_copy(fac, new_fac, sem.at[1])]
    copies[1].start()
    factor_b = fac[...].astype(BF16)
    nt = (((1,), (1,)), ((), ()))
    for i in range(4):
        r = pl.ds(i * 128, 128)
        low_rank = lax.dot_general(ob[r, :], factor_b, nt, preferred_element_type=F32)
        up[r, :] = (math.sqrt(D * FF / RANK) * low_rank).astype(BF16)
        copy = pltpu.make_async_copy(up.at[r], update.at[r], sem.at[2 + i])
        copy.start()
        copies.append(copy)
    for copy in copies:
        copy.wait()


def shards(momentum, gradient, right_factor):
    scratch = [
        pltpu.VMEM((ROWS, COLS), BF16),
        pltpu.VMEM((ROWS, COLS), BF16),
        pltpu.VMEM((COLS, RANK), F32),
        pltpu.VMEM((COLS, RANK), BF16),
        pltpu.VMEM((ROWS, COLS), BF16),
        pltpu.VMEM((HALF, COLS), BF16),
        pltpu.VMEM((ROWS, RANK), BF16),
        pltpu.VMEM((1, 16 * XCH, RANK), BF16),
        pltpu.VMEM((1, HALF, RANK), BF16),
        pltpu.VMEM((1, 8 * XCH, RANK), BF16),
        pltpu.VMEM((2, XCH, RANK), BF16),
        pltpu.VMEM((2, NZ * XCH, RANK), BF16),
        pltpu.VMEM((HALF, RANK), BF16),
        pltpu.VMEM((HALF, RANK), BF16),
        pltpu.VMEM((2, COLS, RANK), BF16),
        pltpu.VMEM((2, 16 * WCH, RANK), BF16),
        pltpu.VMEM((2, WCH, RANK), BF16),
        pltpu.VMEM((2, 16 * WCH, RANK), BF16),
        pltpu.VMEM((2, COLS, RANK), BF16),
        pltpu.VMEM((2, RANK, RANK), F32),
        pltpu.VMEM((2, 16 * GCH, RANK), F32),
        pltpu.VMEM((2, GCH, RANK), F32),
        pltpu.VMEM((1, 16 * GCH, RANK), F32),
        pltpu.VMEM((1, 32 * GCH, RANK), F32),
        pltpu.VMEM((RANK, RANK), F32),
        pltpu.VMEM((2, 1, RANK), F32),
        pltpu.VMEM((NZ, 1, RANK), F32),
        pltpu.VMEM((2 * NZ, 1, RANK), F32),
        pltpu.VMEM((2, RANK, RANK), F32),
        pltpu.VMEM((RANK, RANK), F32),
        pltpu.VMEM((HALF, RANK), F32),
        pltpu.VMEM((10400, RANK), BF16),
        pltpu.SemaphoreType.DMA((5,)),
        pltpu.SemaphoreType.DMA(()),
        pltpu.SemaphoreType.DMA((20,)),
    ]
    arguments = [
        pltpu.with_memory_space_constraint(v, pltpu.HBM)
        for v in (momentum, gradient, right_factor)
    ]
    vmem = pl.BlockSpec(memory_space=pltpu.VMEM)
    anywhere = pl.BlockSpec(memory_space=pl.ANY)
    made = pl.pallas_call(
        kernel,
        out_shape=(
            jax.ShapeDtypeStruct((1, ROWS, COLS), BF16),
            jax.ShapeDtypeStruct((COLS, RANK), F32),
            jax.ShapeDtypeStruct((ROWS, RANK), BF16),
            jax.ShapeDtypeStruct((8, RANK), F32),
        ),
        in_specs=[anywhere] * 3,
        out_specs=(vmem,) * 4,
        scratch_shapes=scratch,
        compiler_params=pltpu.CompilerParams(
            collective_id=0, has_side_effects=True, vmem_limit_bytes=40 * 2**20
        ),
        cost_estimate=pl.CostEstimate(
            flops=10 * ROWS * COLS * RANK, bytes_accessed=4 * 2**20, transcendentals=0
        ),
    )(*arguments)
    return pl.pallas_call(
        finish,
        out_shape=(
            jax.ShapeDtypeStruct((1, ROWS, COLS), BF16),
            jax.ShapeDtypeStruct((ROWS, COLS), BF16),
            jax.ShapeDtypeStruct((COLS, RANK), F32),
        ),
        in_specs=[vmem] * 4,
        out_specs=(anywhere,) * 3,
        scratch_shapes=[
            pltpu.VMEM((COLS, RANK), F32),
            pltpu.VMEM((ROWS, COLS), BF16),
            pltpu.SemaphoreType.DMA((6,)),
        ],
        compiler_params=pltpu.CompilerParams(vmem_limit_bytes=40 * 2**20),
        cost_estimate=pl.CostEstimate(
            flops=2 * ROWS * COLS * RANK, bytes_accessed=3 * 2**20, transcendentals=0
        ),
    )(*made)


def solution(mesh):
    placed = (P("dp", "fsdp", "tensor"), P("dp", "fsdp", "tensor"), P("tensor", None))
    return jax.shard_map(
        shards,
        mesh=mesh,
        in_specs=placed,
        out_specs=(P("dp", "fsdp", "tensor"), P("fsdp", "tensor"), P("tensor", None)),
        check_vma=False,
    )
```

```python
import math

import jax
import jax.numpy as jnp
from jax import lax
from jax.experimental import pallas as pl
from jax.experimental.pallas import tpu as pltpu
from jax.sharding import PartitionSpec as P

D = 8192
FF = 14336
RANK = 128
MESH = pl.DeviceIdType.MESH
F32 = jnp.float32
BF16 = jnp.bfloat16

NZ = 16
ROWS = 512
HALF = 256
COLS = 896
XCH = 32
WCH = 64
GCH = 8
TILES = COLS // 128
PLACES = COLS // WCH
NB = 16

NEAR_Z = [4, 3, -3, 2, -2, 1, -1]
FAR_Z = sorted(range(1, NZ), key=lambda d: -min(d, NZ - d))
NEAR_XY = [(1, 1), (1, 3), (0, 2), (1, 0), (3, 0), (0, 1), (0, 3), (0, 0)]
FAR_XY = sorted(
    [(dx, dy) for dx in range(4) for dy in range(4) if (dx, dy) != (0, 0)],
    key=lambda o: -(min(o[0], 4 - o[0]) + min(o[1], 4 - o[1])),
)


def split3(a):
    high = a.astype(BF16)
    rest = a - high.astype(F32)
    mid = rest.astype(BF16)
    low = (rest - mid.astype(F32)).astype(BF16)
    return high, mid, low


def inverse_cholesky(a_ref, e_ref, panels):
    if panels[0] == 0:
        rows = lax.broadcasted_iota(jnp.int32, (RANK, RANK), 0)
        cols = lax.broadcasted_iota(jnp.int32, (RANK, RANK), 1)
        e_ref[...] = jnp.where(rows == cols, 1.0, 0.0).astype(F32)
    sub = lax.broadcasted_iota(jnp.int32, (NB, RANK), 0)

    def spread(t, j):
        return jnp.broadcast_to(t[j : j + 1, :], (NB, RANK))

    for base in [p * NB for p in panels]:
        last = base + NB
        xa = a_ref[base:last, :]
        xe = e_ref[base:last, :]
        col = [
            jnp.broadcast_to(xa[:, base + k : base + k + 1], (NB, RANK)) for k in range(NB)
        ]
        if last < RANK:
            c1, c2, c3 = split3(a_ref[last:, base:last])
            below = jnp.concatenate([c1, c1, c2, c1, c2, c3], 1)
        inverses = jnp.zeros((NB, RANK), F32)
        out = jnp.zeros((NB, RANK), F32)
        for j in range(NB):
            inv = 1.0 / spread(col[j], j)
            inverses = jnp.where(sub == j, inv, inverses)
            row_e = spread(xe, j)
            out = jnp.where(sub == j, row_e, out)
            factor = jnp.where(sub != j, col[j] * inv, 0.0)
            xa = xa - factor * spread(xa, j)
            xe = xe - factor * row_e
            for k in range(j + 1, NB):
                col[k] = col[k] - factor * spread(col[k], j)
        e_ref[base:last, :] = out * jnp.sqrt(inverses)
        if last < RANK:
            v1, v2, v3 = split3(jnp.concatenate([xa * inverses, xe * inverses], 1))
            solved = jnp.concatenate([v1, v2, v1, v3, v2, v1], 0)
            change = jnp.dot(below, solved, preferred_element_type=F32)
            a_ref[last:, :] = a_ref[last:, :] - change[:, :RANK]
            e_ref[last:, :] = e_ref[last:, :] - change[:, RANK:]


def right_times(tiles_ref, m, first=0, last=TILES):
    parts = jnp.concatenate(split3(m)[:2], 0)
    out = []
    for i in range(first, last):
        tile = tiles_ref[i * 128 : (i + 1) * 128, :]
        r = lax.dot_general(tile, parts, (((0,), (1,)), ((), ())), preferred_element_type=F32)
        out.append(r[:, :RANK] + r[:, RANK:])
    return out


def rows_times(x, m):
    parts = jnp.concatenate(split3(m)[:2], 0)
    r = lax.dot_general(x, parts, (((1,), (1,)), ((), ())), preferred_element_type=F32)
    return r[:, :RANK] + r[:, RANK:]


def kernel(
    mom, grad, fac, new_mom, right, ob, norm,
    m_v, g_v, f_v, fb, own, oth, xs0, xr0, xs1, xr1, xo, xp, xl, xoth, ws, wr, wo, wp, wa, gs, gr, go, gp0, gp1, ga,
    qs, qr0, qr1, lower, a_s, acc, tally, load, send, recv,
):
    c = lax.axis_index("dp")
    f = lax.axis_index("fsdp")
    t = lax.axis_index("tensor")
    x = f // 4
    y = lax.rem(f, 4)
    other = 1 - c
    partner = (other, f, t)

    def core(dc):
        return c if dc == 0 else other

    def along_z(d, dc=0):
        return (core(dc), f, lax.rem(t + d + NZ, NZ))

    def near_z(d, dc=0):
        return along_z(4 + 8 * lax.rem(t, 2) if d == 4 else d, dc)

    def along_xy(dx, dy, dc=0):
        return (core(dc), lax.rem(x + dx, 4) * 4 + lax.rem(y + dy, 4), t)

    def pair_of(chip):
        px = chip // 4
        return lax.rem(px, 2) * 4 + lax.rem(lax.rem(chip, 4) + 2 * (px // 2), 4)

    pair = pair_of(f)
    half = x // 2
    place = c * 8 + pair
    owner = place < PLACES
    idle = jnp.logical_not(owner)
    ring = [along_z(d) for d in FAR_Z]
    chips = [along_xy(*o) for o in FAR_XY]
    near = [(2 * (len(NEAR_XY) - 1 - i) + dc, along_xy(*o, dc)) for i, o in enumerate(NEAR_XY) for dc in (0, 1)]
    near = [(slot, to) for slot, to in near if slot]

    def chunk(index, size):
        return pl.ds(pl.multiple_of(index * size, size), size)

    def put(src, dst, phase, to):
        pltpu.make_async_remote_copy(
            src_ref=src, dst_ref=dst, send_sem=send, recv_sem=recv.at[phase],
            device_id=to, device_id_type=MESH,
        ).start()

    def got(region, phase):
        pltpu.make_async_remote_copy(
            src_ref=region, dst_ref=region, send_sem=send, recv_sem=recv.at[phase],
            device_id=partner, device_id_type=MESH,
        ).wait_recv()

    def all_sent(rows):
        region = tally.at[pl.ds(0, rows)]
        pltpu.make_async_remote_copy(
            src_ref=region, dst_ref=region, send_sem=send, recv_sem=recv.at[0],
            device_id=partner, device_id_type=MESH,
        ).wait_send()

    def summed(ref, it, size, count):
        total = ref[it, 0:size, :].astype(F32)
        for k in range(1, count):
            total = total + ref[it, k * size : (k + 1) * size, :].astype(F32)
        return total

    greet = [along_z(d, dc) for d in (4, -4) for dc in (0, 1)]
    greet += [along_xy(*o, dc) for o in FAR_XY[:5] for dc in (0, 1)]
    greet += [along_z(d, dc) for d in (3, -3, 2, -2, 1, -1) for dc in (0, 1)]
    greet += [along_xy(*o, dc) for o in FAR_XY[5:] for dc in (0, 1)] + [partner]
    barrier = pltpu.get_barrier_semaphore()

    def signal(some):
        for to in some:
            pl.semaphore_signal(barrier, inc=1, device_id=to, device_id_type=MESH)

    signal(greet[:14])
    load_f = pltpu.make_async_copy(fac, f_v, load.at[4])
    load_f.start()
    for i in range(4):
        r = pl.ds(i * 128, 128)
        pair_in = [
            pltpu.make_async_copy(mom.at[0, r], m_v.at[r], load.at[i]),
            pltpu.make_async_copy(grad.at[0, r], g_v.at[r], load.at[i]),
        ]
        for copy in pair_in:
            copy.start()
    signal(greet[14:])
    load_f.wait()
    fb[...] = f_v[...].astype(BF16)
    for i in range(4):
        both = tally.at[pl.ds(0, 2 * 128 * TILES)]
        pltpu.make_async_copy(both, both, load.at[i]).wait()
        r = pl.ds(i * 128, 128)
        block = (m_v[r, :].astype(F32) + g_v[r, :].astype(F32)).astype(BF16)
        own[r, :] = block
        xs0[r, :] = (0.5 * jnp.dot(block, fb[...], preferred_element_type=F32)).astype(BF16)

    mine = pl.ds(pl.multiple_of(c * HALF, HALF), HALF)
    theirs = pl.ds(pl.multiple_of(other * HALF, HALF), HALF)
    nt = (((1,), (1,)), ((), ()))
    tn = (((0,), (0,)), ((), ()))

    def phase(it, k):
        return 2 + 9 * it + k

    def left_spread(it, total):
        xo[it] = total.astype(BF16)
        for to in ring:
            put(xo.at[it], xp.at[it, chunk(t, XCH)], phase(it, 1), to)
        xp[it, chunk(t, XCH), :] = total.astype(BF16)

    def left_here(it):
        got(xp.at[it, pl.ds(0, (NZ - 1) * XCH)], phase(it, 1))
        both = xp[it, 0:HALF, :].astype(F32) + xp[it, HALF : 2 * HALF, :].astype(F32)
        return both.astype(BF16)

    def right_out(it, left):
        part = lax.dot_general(left, own[mine, :], tn, preferred_element_type=F32)
        part = part + lax.dot_general(left, oth[...], tn, preferred_element_type=F32)
        part = (0.5 * part).astype(BF16)
        for i in range(TILES):
            ws[it, i * 128 : (i + 1) * 128, :] = part[:, i * 128 : (i + 1) * 128]
        for slot, to in near:
            there = to[0] * 8 + pair_of(to[1])

            @pl.when(there < PLACES)
            def _():
                put(ws.at[it, chunk(there, WCH)], wr.at[it, pl.ds(slot * WCH, WCH)], phase(it, 2), to)

        @pl.when(owner)
        def _():
            wr[it, 0:WCH, :] = ws[it, chunk(place, WCH), :]

    def right_spread(it):
        @pl.when(owner)
        def _():
            got(wr.at[it, pl.ds(WCH, 15 * WCH)], phase(it, 2))
            total = summed(wr, it, WCH, 16).astype(BF16)
            wo[it] = total
            rows = chunk(half * 8 + pair, WCH)
            for to in chips:
                put(wo.at[it], wp.at[it, rows], phase(it, 3), to)
            wp[it, rows, :] = total

    def right_join(it):
        @pl.when(c == 0)
        def _():
            got(wp.at[it, pl.ds(0, 15 * WCH)], phase(it, 3))
            both = wp[it, 0:512, :].astype(F32) + wp[it, 512:1024, :].astype(F32)
            wa[it, 0:512, :] = both.astype(BF16)
            put(wa.at[it, pl.ds(0, 512)], wa.at[it, pl.ds(0, 512)], phase(it, 4), partner)

        @pl.when(c == 1)
        def _():
            @pl.when(owner)
            def _():
                got(wp.at[it, pl.ds(0, 11 * WCH)], phase(it, 3))

            @pl.when(idle)
            def _():
                got(wp.at[it, pl.ds(0, 12 * WCH)], phase(it, 3))

            both = wp[it, 0:384, :].astype(F32) + wp[it, 512:896, :].astype(F32)
            wa[it, 512:896, :] = both.astype(BF16)
            put(wa.at[it, pl.ds(512, 384)], wa.at[it, pl.ds(512, 384)], phase(it, 4), partner)

    def right_here(it):
        @pl.when(c == 0)
        def _():
            got(wa.at[it, pl.ds(512, 384)], phase(it, 4))

        @pl.when(c == 1)
        def _():
            got(wa.at[it, pl.ds(0, 512)], phase(it, 4))

    def gram_out(it, left):
        gs[it] = lax.dot_general(left, left, tn, preferred_element_type=F32)
        for slot, to in near:
            there = to[0] * 8 + pair_of(to[1])
            put(gs.at[it, chunk(there, GCH)], gr.at[it, pl.ds(slot * GCH, GCH)], phase(it, 5), to)
        gr[it, 0:GCH, :] = gs[it, chunk(place, GCH), :]

    def gram_owned(it):
        got(gr.at[it, pl.ds(GCH, 15 * GCH)], phase(it, 5))
        total = summed(gr, it, GCH, 16)
        go[it] = total
        return total

    def gram_spread_core(total):
        rows = chunk(half * 8 + pair, GCH)
        for to in chips:
            put(go.at[0], gp0.at[0, rows], phase(0, 6), to)
        gp0[0, rows, :] = total

    def gram_join_core():
        got(gp0.at[0, pl.ds(0, 15 * GCH)], phase(0, 6))
        rows = chunk(c, RANK // 2)
        ga[rows, :] = gp0[0, 0 : RANK // 2, :] + gp0[0, RANK // 2 : RANK, :]
        put(ga.at[rows], ga.at[rows], phase(0, 8), partner)
        got(ga.at[pl.ds(0, RANK // 2)], phase(0, 8))
        return ga[...]

    def gram_spread_all(total):
        rows = chunk(half * 16 + place, GCH)
        for o in FAR_XY:
            for dc in (0, 1):
                put(go.at[1], gp1.at[0, rows], phase(1, 6), along_xy(*o, dc))
        put(go.at[1], gp1.at[0, rows], phase(1, 6), partner)
        gp1[0, rows, :] = total

    def gram_join_all():
        got(gp1.at[0, pl.ds(0, 31 * GCH)], phase(1, 6))
        return gp1[0, 0:RANK, :] + gp1[0, RANK : 2 * RANK, :]

    def squares_sum(it, tiles):
        total = jnp.sum(tiles[0] * tiles[0], axis=0, keepdims=True)
        for tile in tiles[1:]:
            total = total + jnp.sum(tile * tile, axis=0, keepdims=True)
        qs[it] = total

    def squares_send_core():
        for to in ring:
            put(qs.at[0], qr0.at[t], phase(0, 7), to)
        qr0[t] = qs[0]

    def squares_send_all():
        slot = 2 * t + c
        for d in FAR_Z:
            for dc in (0, 1):
                put(qs.at[1], qr1.at[slot], phase(1, 7), along_z(d, dc))
        put(qs.at[1], qr1.at[slot], phase(1, 7), partner)
        qr1[slot] = qs[1]

    def norms(it):
        ref, count = (qr0, NZ) if it == 0 else (qr1, 2 * NZ)
        got(ref.at[pl.ds(0, count - 1)], phase(it, 7))
        total = ref[0]
        for k in range(1, count):
            total = total + ref[k]
        return jnp.sqrt(total + 1e-06)

    pl.semaphore_wait(barrier, len(greet))
    for d in NEAR_Z + [0]:
        for dc in (0, 1):
            if (d, dc) == (0, 0):
                continue
            to = near_z(d, dc)
            src = xs0.at[chunk(to[0] * 8 + lax.rem(to[2], 8), XCH)]
            put(src, xr0.at[0, pl.ds((2 * (d % 8) + dc) * XCH, XCH)], phase(0, 0), to)
    xr0[0, 0:XCH, :] = xs0[chunk(c * 8 + lax.rem(t, 8), XCH), :]
    got(xr0.at[0, pl.ds(XCH, 15 * XCH)], phase(0, 0))
    left_spread(0, summed(xr0, 0, XCH, 16))
    put(own.at[theirs], oth, 0, partner)
    got(oth, 0)
    left = left_here(0)
    right_out(0, left)
    gram_out(0, left)
    right_spread(0)
    gram_spread_core(gram_owned(0))
    right_join(0)

    def products(first, last):
        tiles = [wa[0, i * 128 : (i + 1) * 128, :] for i in range(first, last)]
        tiles = jnp.concatenate(tiles, 1)
        cols = pl.ds(first * 128, (last - first) * 128)
        part = lax.dot_general(own[mine, cols], tiles, nt, preferred_element_type=F32)
        return part + lax.dot_general(oth[:, cols], tiles, nt, preferred_element_type=F32)

    @pl.when(c == 0)
    def _():
        acc[...] = products(0, 4)

    @pl.when(c == 1)
    def _():
        acc[...] = products(4, 7)

    right_here(0)

    @pl.when(c == 0)
    def _():
        xs1[0] = (0.5 * (acc[...] + products(4, 7))).astype(BF16)

    @pl.when(c == 1)
    def _():
        xs1[0] = (0.5 * (acc[...] + products(0, 4))).astype(BF16)

    for d in NEAR_Z:
        to = near_z(d)
        src = xs1.at[0, chunk(lax.rem(to[2], 8), XCH)]
        put(src, xr1.at[0, pl.ds((d % 8) * XCH, XCH)], phase(1, 0), to)
    xr1[0, 0:XCH, :] = xs1[0, chunk(lax.rem(t, 8), XCH), :]
    a_s[...] = gram_join_core()
    inverse_cholesky(a_s, lower.at[0], range(8))
    low_parts = split3(lower[0])
    low_parts = jnp.concatenate([low_parts[0], low_parts[1], low_parts[0]], 1)
    got(xr1.at[0, pl.ds(XCH, 7 * XCH)], phase(1, 0))
    owned = split3(summed(xr1, 0, XCH, 8))
    owned = jnp.concatenate([owned[0], owned[0], owned[1]], 1)
    left_spread(1, lax.dot_general(owned, low_parts, nt, preferred_element_type=F32))
    squares_sum(0, right_times(wa.at[0], lower[0]))
    left = left_here(1)
    gram_out(1, left)
    squares_send_core()
    xl[...] = left
    put(xl, xoth, 1, partner)
    right_out(1, left)
    gram_spread_all(gram_owned(1))
    right_spread(1)
    scale = jnp.broadcast_to(1.0 / norms(0), (RANK, RANK))
    a_s[...] = scale * scale.T
    a_s[...] = gram_join_all() * a_s[...]
    inverse_cholesky(a_s, lower.at[1], range(8))
    mix = lower[1] * scale
    right_join(1)

    def right_tiles(first, last):
        tiles = right_times(wa.at[1], mix, first, last)
        for i in range(first, last):
            right[i * 128 : (i + 1) * 128, :] = tiles[i - first]
        return tiles

    @pl.when(c == 0)
    def _():
        squares_sum(1, right_tiles(0, 4))

    @pl.when(c == 1)
    def _():
        squares_sum(1, right_tiles(4, 7))

    squares_send_all()
    right_here(1)

    @pl.when(c == 0)
    def _():
        right_tiles(4, 7)

    @pl.when(c == 1)
    def _():
        right_tiles(0, 4)

    got(xoth, 1)
    ob[mine, :] = rows_times(xl[...], mix).astype(BF16)
    ob[theirs, :] = rows_times(xoth[...], mix).astype(BF16)
    right_b = right[...].astype(BF16)
    for i in range(4):
        r = pl.ds(i * 128, 128)
        feedback = lax.dot_general(ob[r, :], right_b, nt, preferred_element_type=F32)
        new_mom[0, r, :] = (own[r, :].astype(F32) - 0.05 * feedback).astype(BF16)

    everyone = 1792 + 256 + 480 + 224 + 2 * 480 + 2 * 240 + 240 + 496 + 128 + 30 + 62

    @pl.when(c == 0)
    def _():
        all_sent(everyone + 2 * (13 * WCH + 15 * WCH + 512))

    @pl.when((c == 1) & owner)
    def _():
        all_sent(everyone + 2 * (13 * WCH + 15 * WCH + 384))

    @pl.when(idle)
    def _():
        all_sent(everyone + 2 * (14 * WCH + 384))

    norm[...] = jnp.broadcast_to(1.0 / norms(1), (8, RANK))


def finish(new_mom, right, ob, norm, new_mom_out, update, new_fac, fac, up, sem):
    first = pltpu.make_async_copy(new_mom, new_mom_out, sem.at[0])
    first.start()
    fac[...] = right[...] * norm[0:1, :]
    copies = [first, pltpu.make_async_copy(fac, new_fac, sem.at[1])]
    copies[1].start()
    factor_b = fac[...].astype(BF16)
    nt = (((1,), (1,)), ((), ()))
    for i in range(4):
        r = pl.ds(i * 128, 128)
        low_rank = lax.dot_general(ob[r, :], factor_b, nt, preferred_element_type=F32)
        up[r, :] = (math.sqrt(D * FF / RANK) * low_rank).astype(BF16)
        copy = pltpu.make_async_copy(up.at[r], update.at[r], sem.at[2 + i])
        copy.start()
        copies.append(copy)
    for copy in copies:
        copy.wait()


def shards(momentum, gradient, right_factor):
    scratch = [
        pltpu.VMEM((ROWS, COLS), BF16),
        pltpu.VMEM((ROWS, COLS), BF16),
        pltpu.VMEM((COLS, RANK), F32),
        pltpu.VMEM((COLS, RANK), BF16),
        pltpu.VMEM((ROWS, COLS), BF16),
        pltpu.VMEM((HALF, COLS), BF16),
        pltpu.VMEM((ROWS, RANK), BF16),
        pltpu.VMEM((1, 16 * XCH, RANK), BF16),
        pltpu.VMEM((1, HALF, RANK), BF16),
        pltpu.VMEM((1, 8 * XCH, RANK), BF16),
        pltpu.VMEM((2, XCH, RANK), BF16),
        pltpu.VMEM((2, NZ * XCH, RANK), BF16),
        pltpu.VMEM((HALF, RANK), BF16),
        pltpu.VMEM((HALF, RANK), BF16),
        pltpu.VMEM((2, COLS, RANK), BF16),
        pltpu.VMEM((2, 16 * WCH, RANK), BF16),
        pltpu.VMEM((2, WCH, RANK), BF16),
        pltpu.VMEM((2, 16 * WCH, RANK), BF16),
        pltpu.VMEM((2, COLS, RANK), BF16),
        pltpu.VMEM((2, RANK, RANK), F32),
        pltpu.VMEM((2, 16 * GCH, RANK), F32),
        pltpu.VMEM((2, GCH, RANK), F32),
        pltpu.VMEM((1, 16 * GCH, RANK), F32),
        pltpu.VMEM((1, 32 * GCH, RANK), F32),
        pltpu.VMEM((RANK, RANK), F32),
        pltpu.VMEM((2, 1, RANK), F32),
        pltpu.VMEM((NZ, 1, RANK), F32),
        pltpu.VMEM((2 * NZ, 1, RANK), F32),
        pltpu.VMEM((2, RANK, RANK), F32),
        pltpu.VMEM((RANK, RANK), F32),
        pltpu.VMEM((HALF, RANK), F32),
        pltpu.VMEM((10400, RANK), BF16),
        pltpu.SemaphoreType.DMA((5,)),
        pltpu.SemaphoreType.DMA(()),
        pltpu.SemaphoreType.DMA((20,)),
    ]
    arguments = [
        pltpu.with_memory_space_constraint(v, pltpu.HBM)
        for v in (momentum, gradient, right_factor)
    ]
    vmem = pl.BlockSpec(memory_space=pltpu.VMEM)
    anywhere = pl.BlockSpec(memory_space=pl.ANY)
    made = pl.pallas_call(
        kernel,
        out_shape=(
            jax.ShapeDtypeStruct((1, ROWS, COLS), BF16),
            jax.ShapeDtypeStruct((COLS, RANK), F32),
            jax.ShapeDtypeStruct((ROWS, RANK), BF16),
            jax.ShapeDtypeStruct((8, RANK), F32),
        ),
        in_specs=[anywhere] * 3,
        out_specs=(vmem,) * 4,
        scratch_shapes=scratch,
        compiler_params=pltpu.CompilerParams(
            collective_id=0, has_side_effects=True, vmem_limit_bytes=40 * 2**20
        ),
        cost_estimate=pl.CostEstimate(
            flops=10 * ROWS * COLS * RANK, bytes_accessed=4 * 2**20, transcendentals=0
        ),
    )(*arguments)
    return pl.pallas_call(
        finish,
        out_shape=(
            jax.ShapeDtypeStruct((1, ROWS, COLS), BF16),
            jax.ShapeDtypeStruct((ROWS, COLS), BF16),
            jax.ShapeDtypeStruct((COLS, RANK), F32),
        ),
        in_specs=[vmem] * 4,
        out_specs=(anywhere,) * 3,
        scratch_shapes=[
            pltpu.VMEM((COLS, RANK), F32),
            pltpu.VMEM((ROWS, COLS), BF16),
            pltpu.SemaphoreType.DMA((6,)),
        ],
        compiler_params=pltpu.CompilerParams(vmem_limit_bytes=40 * 2**20),
        cost_estimate=pl.CostEstimate(
            flops=2 * ROWS * COLS * RANK, bytes_accessed=3 * 2**20, transcendentals=0
        ),
    )(*made)


def solution(mesh):
    placed = (P("dp", "fsdp", "tensor"), P("dp", "fsdp", "tensor"), P("tensor", None))
    return jax.shard_map(
        shards,
        mesh=mesh,
        in_specs=placed,
        out_specs=(P("dp", "fsdp", "tensor"), P("fsdp", "tensor"), P("tensor", None)),
        check_vma=False,
    )
```

```python
import math

import jax
import jax.numpy as jnp
from jax import lax
from jax.experimental import pallas as pl
from jax.experimental.pallas import tpu as pltpu
from jax.sharding import PartitionSpec as P

D = 8192
FF = 14336
RANK = 128
MESH = pl.DeviceIdType.MESH
F32 = jnp.float32
BF16 = jnp.bfloat16

NZ = 16
ROWS = 512
HALF = 256
COLS = 896
XCH = 32
WCH = 64
GCH = 8
TILES = COLS // 128
PLACES = COLS // WCH
NB = 16

NEAR_Z = [4, 3, -3, 2, -2, 1, -1]
FAR_Z = sorted(range(1, NZ), key=lambda d: -min(d, NZ - d))
NEAR_XY = [(1, 1), (1, 3), (0, 2), (1, 0), (3, 0), (0, 1), (0, 3), (0, 0)]
FAR_XY = sorted(
    [(dx, dy) for dx in range(4) for dy in range(4) if (dx, dy) != (0, 0)],
    key=lambda o: -(min(o[0], 4 - o[0]) + min(o[1], 4 - o[1])),
)


def split3(a):
    high = a.astype(BF16)
    rest = a - high.astype(F32)
    mid = rest.astype(BF16)
    low = (rest - mid.astype(F32)).astype(BF16)
    return high, mid, low


def inverse_cholesky(a_ref, e_ref, panels):
    if panels[0] == 0:
        rows = lax.broadcasted_iota(jnp.int32, (RANK, RANK), 0)
        cols = lax.broadcasted_iota(jnp.int32, (RANK, RANK), 1)
        e_ref[...] = jnp.where(rows == cols, 1.0, 0.0).astype(F32)
    sub = lax.broadcasted_iota(jnp.int32, (NB, RANK), 0)

    def spread(t, j):
        return jnp.broadcast_to(t[j : j + 1, :], (NB, RANK))

    for base in [p * NB for p in panels]:
        last = base + NB
        xa = a_ref[base:last, :]
        xe = e_ref[base:last, :]
        col = [
            jnp.broadcast_to(xa[:, base + k : base + k + 1], (NB, RANK)) for k in range(NB)
        ]
        if last < RANK:
            c1, c2, c3 = split3(a_ref[last:, base:last])
            below = jnp.concatenate([c1, c1, c2, c1, c2, c3], 1)
        inverses = jnp.zeros((NB, RANK), F32)
        out = jnp.zeros((NB, RANK), F32)
        for j in range(NB):
            inv = 1.0 / spread(col[j], j)
            inverses = jnp.where(sub == j, inv, inverses)
            row_e = spread(xe, j)
            out = jnp.where(sub == j, row_e, out)
            factor = jnp.where(sub != j, col[j] * inv, 0.0)
            xa = xa - factor * spread(xa, j)
            xe = xe - factor * row_e
            for k in range(j + 1, NB):
                col[k] = col[k] - factor * spread(col[k], j)
        e_ref[base:last, :] = out * jnp.sqrt(inverses)
        if last < RANK:
            v1, v2, v3 = split3(jnp.concatenate([xa * inverses, xe * inverses], 1))
            solved = jnp.concatenate([v1, v2, v1, v3, v2, v1], 0)
            change = jnp.dot(below, solved, preferred_element_type=F32)
            a_ref[last:, :] = a_ref[last:, :] - change[:, :RANK]
            e_ref[last:, :] = e_ref[last:, :] - change[:, RANK:]


def right_times(tiles_ref, m, first=0, last=TILES):
    parts = jnp.concatenate(split3(m)[:2], 0)
    out = []
    for i in range(first, last):
        tile = tiles_ref[i * 128 : (i + 1) * 128, :]
        r = lax.dot_general(tile, parts, (((0,), (1,)), ((), ())), preferred_element_type=F32)
        out.append(r[:, :RANK] + r[:, RANK:])
    return out


def rows_times(x, m):
    parts = jnp.concatenate(split3(m)[:2], 0)
    r = lax.dot_general(x, parts, (((1,), (1,)), ((), ())), preferred_element_type=F32)
    return r[:, :RANK] + r[:, RANK:]


def kernel(
    mom, grad, fac, new_mom, right, ob, norm,
    m_v, g_v, f_v, fb, own, oth, xs0, xr0, xs1, xr1, xo, xp, xl, xoth, ws, wr, wo, wp, wa, gs, gr, go, gp0, gp1, ga,
    qs, qr0, qr1, lower, a_s, acc, tally, load, send, recv,
):
    c = lax.axis_index("dp")
    f = lax.axis_index("fsdp")
    t = lax.axis_index("tensor")
    x = f // 4
    y = lax.rem(f, 4)
    other = 1 - c
    partner = (other, f, t)

    def core(dc):
        return c if dc == 0 else other

    def along_z(d, dc=0):
        return (core(dc), f, lax.rem(t + d + NZ, NZ))

    def near_z(d, dc=0):
        return along_z(4 + 8 * lax.rem(t, 2) if d == 4 else d, dc)

    def along_xy(dx, dy, dc=0):
        return (core(dc), lax.rem(x + dx, 4) * 4 + lax.rem(y + dy, 4), t)

    def pair_of(chip):
        px = chip // 4
        return lax.rem(px, 2) * 4 + lax.rem(lax.rem(chip, 4) + 2 * (px // 2), 4)

    pair = pair_of(f)
    half = x // 2
    place = c * 8 + pair
    owner = place < PLACES
    idle = jnp.logical_not(owner)
    ring = [along_z(d) for d in FAR_Z]
    chips = [along_xy(*o) for o in FAR_XY]
    near = [(2 * (len(NEAR_XY) - 1 - i) + dc, along_xy(*o, dc)) for i, o in enumerate(NEAR_XY) for dc in (0, 1)]
    near = [(slot, to) for slot, to in near if slot]

    def chunk(index, size):
        return pl.ds(pl.multiple_of(index * size, size), size)

    def put(src, dst, phase, to, group=0):
        pltpu.make_async_remote_copy(
            src_ref=src, dst_ref=dst, send_sem=send.at[group], recv_sem=recv.at[phase],
            device_id=to, device_id_type=MESH,
        ).start()

    def got(region, phase):
        pltpu.make_async_remote_copy(
            src_ref=region, dst_ref=region, send_sem=send.at[0], recv_sem=recv.at[phase],
            device_id=partner, device_id_type=MESH,
        ).wait_recv()

    def all_sent(region, group):
        pltpu.make_async_remote_copy(
            src_ref=region, dst_ref=region, send_sem=send.at[group], recv_sem=recv.at[0],
            device_id=partner, device_id_type=MESH,
        ).wait_send()

    def summed(ref, it, size, count):
        total = ref[it, 0:size, :].astype(F32)
        for k in range(1, count):
            total = total + ref[it, k * size : (k + 1) * size, :].astype(F32)
        return total

    greet = [along_z(d, dc) for d in (4, -4) for dc in (0, 1)]
    greet += [along_xy(*o, dc) for o in FAR_XY[:5] for dc in (0, 1)]
    greet += [along_z(d, dc) for d in (3, -3, 2, -2, 1, -1) for dc in (0, 1)]
    greet += [along_xy(*o, dc) for o in FAR_XY[5:] for dc in (0, 1)] + [partner]
    barrier = pltpu.get_barrier_semaphore()

    def signal(some):
        for to in some:
            pl.semaphore_signal(barrier, inc=1, device_id=to, device_id_type=MESH)

    signal(greet[:14])
    load_f = pltpu.make_async_copy(fac, f_v, load.at[4])
    load_f.start()
    for i in range(4):
        r = pl.ds(i * 128, 128)
        pair_in = [
            pltpu.make_async_copy(mom.at[0, r], m_v.at[r], load.at[i]),
            pltpu.make_async_copy(grad.at[0, r], g_v.at[r], load.at[i]),
        ]
        for copy in pair_in:
            copy.start()
    signal(greet[14:])
    load_f.wait()
    fb[...] = f_v[...].astype(BF16)
    for i in range(4):
        both = tally.at[pl.ds(0, 2 * 128 * TILES)]
        pltpu.make_async_copy(both, both, load.at[i]).wait()
        r = pl.ds(i * 128, 128)
        block = (m_v[r, :].astype(F32) + g_v[r, :].astype(F32)).astype(BF16)
        own[r, :] = block
        xs0[r, :] = (0.5 * jnp.dot(block, fb[...], preferred_element_type=F32)).astype(BF16)

    mine = pl.ds(pl.multiple_of(c * HALF, HALF), HALF)
    theirs = pl.ds(pl.multiple_of(other * HALF, HALF), HALF)
    nt = (((1,), (1,)), ((), ()))
    tn = (((0,), (0,)), ((), ()))

    def phase(it, k):
        return 2 + 9 * it + k

    def left_spread(it, total):
        xo[it] = total.astype(BF16)
        for to in ring:
            put(xo.at[it], xp.at[it, chunk(t, XCH)], phase(it, 1), to)
        xp[it, chunk(t, XCH), :] = total.astype(BF16)

    def left_here(it):
        got(xp.at[it, pl.ds(0, (NZ - 1) * XCH)], phase(it, 1))
        both = xp[it, 0:HALF, :].astype(F32) + xp[it, HALF : 2 * HALF, :].astype(F32)
        return both.astype(BF16)

    def right_out(it, left):
        part = lax.dot_general(left, own[mine, :], tn, preferred_element_type=F32)
        part = part + lax.dot_general(left, oth[...], tn, preferred_element_type=F32)
        part = (0.5 * part).astype(BF16)
        for i in range(TILES):
            ws[it, i * 128 : (i + 1) * 128, :] = part[:, i * 128 : (i + 1) * 128]
        for slot, to in near:
            there = to[0] * 8 + pair_of(to[1])

            @pl.when(there < PLACES)
            def _():
                put(ws.at[it, chunk(there, WCH)], wr.at[it, pl.ds(slot * WCH, WCH)], phase(it, 2), to)

        @pl.when(owner)
        def _():
            wr[it, 0:WCH, :] = ws[it, chunk(place, WCH), :]

    def right_spread(it):
        @pl.when(owner)
        def _():
            got(wr.at[it, pl.ds(WCH, 15 * WCH)], phase(it, 2))
            total = summed(wr, it, WCH, 16).astype(BF16)
            wo[it] = total
            rows = chunk(half * 8 + pair, WCH)
            for to in chips:
                put(wo.at[it], wp.at[it, rows], phase(it, 3), to)
            wp[it, rows, :] = total

    def right_join(it):
        @pl.when(c == 0)
        def _():
            got(wp.at[it, pl.ds(0, 15 * WCH)], phase(it, 3))
            both = wp[it, 0:512, :].astype(F32) + wp[it, 512:1024, :].astype(F32)
            wa[it, 0:512, :] = both.astype(BF16)
            put(wa.at[it, pl.ds(0, 512)], wa.at[it, pl.ds(0, 512)], phase(it, 4), partner)

        @pl.when(c == 1)
        def _():
            @pl.when(owner)
            def _():
                got(wp.at[it, pl.ds(0, 11 * WCH)], phase(it, 3))

            @pl.when(idle)
            def _():
                got(wp.at[it, pl.ds(0, 12 * WCH)], phase(it, 3))

            both = wp[it, 0:384, :].astype(F32) + wp[it, 512:896, :].astype(F32)
            wa[it, 512:896, :] = both.astype(BF16)
            put(wa.at[it, pl.ds(512, 384)], wa.at[it, pl.ds(512, 384)], phase(it, 4), partner)

    def right_here(it):
        @pl.when(c == 0)
        def _():
            got(wa.at[it, pl.ds(512, 384)], phase(it, 4))

        @pl.when(c == 1)
        def _():
            got(wa.at[it, pl.ds(0, 512)], phase(it, 4))

    def gram_out(it, left):
        gs[it] = lax.dot_general(left, left, tn, preferred_element_type=F32)
        for slot, to in near:
            there = to[0] * 8 + pair_of(to[1])
            put(gs.at[it, chunk(there, GCH)], gr.at[it, pl.ds(slot * GCH, GCH)], phase(it, 5), to)
        gr[it, 0:GCH, :] = gs[it, chunk(place, GCH), :]

    def gram_owned(it):
        got(gr.at[it, pl.ds(GCH, 15 * GCH)], phase(it, 5))
        total = summed(gr, it, GCH, 16)
        go[it] = total
        return total

    def gram_spread_core(total):
        rows = chunk(half * 8 + pair, GCH)
        for to in chips:
            put(go.at[0], gp0.at[0, rows], phase(0, 6), to)
        gp0[0, rows, :] = total

    def gram_join_core():
        got(gp0.at[0, pl.ds(0, 15 * GCH)], phase(0, 6))
        rows = chunk(c, RANK // 2)
        ga[rows, :] = gp0[0, 0 : RANK // 2, :] + gp0[0, RANK // 2 : RANK, :]
        put(ga.at[rows], ga.at[rows], phase(0, 8), partner)
        got(ga.at[pl.ds(0, RANK // 2)], phase(0, 8))
        return ga[...]

    def gram_spread_all(total):
        rows = chunk(half * 16 + place, GCH)
        for o in FAR_XY:
            for dc in (0, 1):
                put(go.at[1], gp1.at[0, rows], phase(1, 6), along_xy(*o, dc))
        put(go.at[1], gp1.at[0, rows], phase(1, 6), partner)
        gp1[0, rows, :] = total

    def gram_join_all():
        got(gp1.at[0, pl.ds(0, 31 * GCH)], phase(1, 6))
        return gp1[0, 0:RANK, :] + gp1[0, RANK : 2 * RANK, :]

    def squares_sum(it, tiles):
        total = jnp.sum(tiles[0] * tiles[0], axis=0, keepdims=True)
        for tile in tiles[1:]:
            total = total + jnp.sum(tile * tile, axis=0, keepdims=True)
        qs[it] = total

    def squares_send_core():
        for to in ring:
            put(qs.at[0], qr0.at[t], phase(0, 7), to, 1)
        qr0[t] = qs[0]

    def squares_send_all():
        slot = 2 * t + c
        for d in FAR_Z:
            for dc in (0, 1):
                put(qs.at[1], qr1.at[slot], phase(1, 7), along_z(d, dc), 2)
        put(qs.at[1], qr1.at[slot], phase(1, 7), partner, 2)
        qr1[slot] = qs[1]

    def norms(it):
        ref, count = (qr0, NZ) if it == 0 else (qr1, 2 * NZ)
        got(ref.at[pl.ds(0, count - 1)], phase(it, 7))
        total = ref[0]
        for k in range(1, count):
            total = total + ref[k]
        return jnp.sqrt(total + 1e-06)

    pl.semaphore_wait(barrier, len(greet))
    for d in NEAR_Z + [0]:
        for dc in (0, 1):
            if (d, dc) == (0, 0):
                continue
            to = near_z(d, dc)
            src = xs0.at[chunk(to[0] * 8 + lax.rem(to[2], 8), XCH)]
            put(src, xr0.at[0, pl.ds((2 * (d % 8) + dc) * XCH, XCH)], phase(0, 0), to)
    xr0[0, 0:XCH, :] = xs0[chunk(c * 8 + lax.rem(t, 8), XCH), :]
    got(xr0.at[0, pl.ds(XCH, 15 * XCH)], phase(0, 0))
    left_spread(0, summed(xr0, 0, XCH, 16))
    put(own.at[theirs], oth, 0, partner)
    got(oth, 0)
    left = left_here(0)
    right_out(0, left)
    gram_out(0, left)
    right_spread(0)
    gram_spread_core(gram_owned(0))
    right_join(0)

    def products(first, last):
        tiles = [wa[0, i * 128 : (i + 1) * 128, :] for i in range(first, last)]
        tiles = jnp.concatenate(tiles, 1)
        cols = pl.ds(first * 128, (last - first) * 128)
        part = lax.dot_general(own[mine, cols], tiles, nt, preferred_element_type=F32)
        return part + lax.dot_general(oth[:, cols], tiles, nt, preferred_element_type=F32)

    @pl.when(c == 0)
    def _():
        acc[...] = products(0, 4)

    @pl.when(c == 1)
    def _():
        acc[...] = products(4, 7)

    right_here(0)

    @pl.when(c == 0)
    def _():
        xs1[0] = (0.5 * (acc[...] + products(4, 7))).astype(BF16)

    @pl.when(c == 1)
    def _():
        xs1[0] = (0.5 * (acc[...] + products(0, 4))).astype(BF16)

    for d in NEAR_Z:
        to = near_z(d)
        src = xs1.at[0, chunk(lax.rem(to[2], 8), XCH)]
        put(src, xr1.at[0, pl.ds((d % 8) * XCH, XCH)], phase(1, 0), to)
    xr1[0, 0:XCH, :] = xs1[0, chunk(lax.rem(t, 8), XCH), :]
    a_s[...] = gram_join_core()
    inverse_cholesky(a_s, lower.at[0], range(8))
    low_parts = split3(lower[0])
    low_parts = jnp.concatenate([low_parts[0], low_parts[1], low_parts[0]], 1)
    got(xr1.at[0, pl.ds(XCH, 7 * XCH)], phase(1, 0))
    owned = split3(summed(xr1, 0, XCH, 8))
    owned = jnp.concatenate([owned[0], owned[0], owned[1]], 1)
    left_spread(1, lax.dot_general(owned, low_parts, nt, preferred_element_type=F32))
    squares_sum(0, right_times(wa.at[0], lower[0]))
    left = left_here(1)
    gram_out(1, left)
    squares_send_core()
    xl[...] = left
    put(xl, xoth, 1, partner)
    right_out(1, left)
    gram_spread_all(gram_owned(1))
    right_spread(1)
    scale = jnp.broadcast_to(1.0 / norms(0), (RANK, RANK))
    a_s[...] = scale * scale.T
    a_s[...] = gram_join_all() * a_s[...]
    inverse_cholesky(a_s, lower.at[1], range(8))
    mix = lower[1] * scale
    right_join(1)

    def right_tiles(first, last):
        tiles = right_times(wa.at[1], mix, first, last)
        for i in range(first, last):
            right[i * 128 : (i + 1) * 128, :] = tiles[i - first]
        return tiles

    @pl.when(c == 0)
    def _():
        squares_sum(1, right_tiles(0, 4))

    @pl.when(c == 1)
    def _():
        squares_sum(1, right_tiles(4, 7))

    squares_send_all()
    right_here(1)

    @pl.when(c == 0)
    def _():
        right_tiles(4, 7)

    @pl.when(c == 1)
    def _():
        right_tiles(0, 4)

    got(xoth, 1)
    ob[mine, :] = rows_times(xl[...], mix).astype(BF16)
    ob[theirs, :] = rows_times(xoth[...], mix).astype(BF16)
    right_b = right[...].astype(BF16)
    for i in range(4):
        r = pl.ds(i * 128, 128)
        feedback = lax.dot_general(ob[r, :], right_b, nt, preferred_element_type=F32)
        new_mom[0, r, :] = (own[r, :].astype(F32) - 0.05 * feedback).astype(BF16)

    all_sent(qr0.at[pl.ds(0, NZ - 1)], 1)
    all_sent(qr1.at[pl.ds(0, 2 * NZ - 1)], 2)
    everyone = 1792 + 256 + 480 + 224 + 2 * 480 + 2 * 240 + 240 + 496 + 128

    @pl.when(c == 0)
    def _():
        all_sent(tally.at[pl.ds(0, everyone + 2 * (13 * WCH + 15 * WCH + 512))], 0)

    @pl.when((c == 1) & owner)
    def _():
        all_sent(tally.at[pl.ds(0, everyone + 2 * (13 * WCH + 15 * WCH + 384))], 0)

    @pl.when(idle)
    def _():
        all_sent(tally.at[pl.ds(0, everyone + 2 * (14 * WCH + 384))], 0)

    norm[...] = jnp.broadcast_to(1.0 / norms(1), (8, RANK))


def finish(new_mom, right, ob, norm, new_mom_out, update, new_fac, fac, up, sem):
    first = pltpu.make_async_copy(new_mom, new_mom_out, sem.at[0])
    first.start()
    fac[...] = right[...] * norm[0:1, :]
    copies = [first, pltpu.make_async_copy(fac, new_fac, sem.at[1])]
    copies[1].start()
    factor_b = fac[...].astype(BF16)
    nt = (((1,), (1,)), ((), ()))
    for i in range(4):
        r = pl.ds(i * 128, 128)
        low_rank = lax.dot_general(ob[r, :], factor_b, nt, preferred_element_type=F32)
        up[r, :] = (math.sqrt(D * FF / RANK) * low_rank).astype(BF16)
        copy = pltpu.make_async_copy(up.at[r], update.at[r], sem.at[2 + i])
        copy.start()
        copies.append(copy)
    for copy in copies:
        copy.wait()


def shards(momentum, gradient, right_factor):
    scratch = [
        pltpu.VMEM((ROWS, COLS), BF16),
        pltpu.VMEM((ROWS, COLS), BF16),
        pltpu.VMEM((COLS, RANK), F32),
        pltpu.VMEM((COLS, RANK), BF16),
        pltpu.VMEM((ROWS, COLS), BF16),
        pltpu.VMEM((HALF, COLS), BF16),
        pltpu.VMEM((ROWS, RANK), BF16),
        pltpu.VMEM((1, 16 * XCH, RANK), BF16),
        pltpu.VMEM((1, HALF, RANK), BF16),
        pltpu.VMEM((1, 8 * XCH, RANK), BF16),
        pltpu.VMEM((2, XCH, RANK), BF16),
        pltpu.VMEM((2, NZ * XCH, RANK), BF16),
        pltpu.VMEM((HALF, RANK), BF16),
        pltpu.VMEM((HALF, RANK), BF16),
        pltpu.VMEM((2, COLS, RANK), BF16),
        pltpu.VMEM((2, 16 * WCH, RANK), BF16),
        pltpu.VMEM((2, WCH, RANK), BF16),
        pltpu.VMEM((2, 16 * WCH, RANK), BF16),
        pltpu.VMEM((2, COLS, RANK), BF16),
        pltpu.VMEM((2, RANK, RANK), F32),
        pltpu.VMEM((2, 16 * GCH, RANK), F32),
        pltpu.VMEM((2, GCH, RANK), F32),
        pltpu.VMEM((1, 16 * GCH, RANK), F32),
        pltpu.VMEM((1, 32 * GCH, RANK), F32),
        pltpu.VMEM((RANK, RANK), F32),
        pltpu.VMEM((2, 1, RANK), F32),
        pltpu.VMEM((NZ, 1, RANK), F32),
        pltpu.VMEM((2 * NZ, 1, RANK), F32),
        pltpu.VMEM((2, RANK, RANK), F32),
        pltpu.VMEM((RANK, RANK), F32),
        pltpu.VMEM((HALF, RANK), F32),
        pltpu.VMEM((10400, RANK), BF16),
        pltpu.SemaphoreType.DMA((5,)),
        pltpu.SemaphoreType.DMA((3,)),
        pltpu.SemaphoreType.DMA((20,)),
    ]
    arguments = [
        pltpu.with_memory_space_constraint(v, pltpu.HBM)
        for v in (momentum, gradient, right_factor)
    ]
    vmem = pl.BlockSpec(memory_space=pltpu.VMEM)
    anywhere = pl.BlockSpec(memory_space=pl.ANY)
    made = pl.pallas_call(
        kernel,
        out_shape=(
            jax.ShapeDtypeStruct((1, ROWS, COLS), BF16),
            jax.ShapeDtypeStruct((COLS, RANK), F32),
            jax.ShapeDtypeStruct((ROWS, RANK), BF16),
            jax.ShapeDtypeStruct((8, RANK), F32),
        ),
        in_specs=[anywhere] * 3,
        out_specs=(vmem,) * 4,
        scratch_shapes=scratch,
        compiler_params=pltpu.CompilerParams(
            collective_id=0, has_side_effects=True, vmem_limit_bytes=40 * 2**20
        ),
        cost_estimate=pl.CostEstimate(
            flops=10 * ROWS * COLS * RANK, bytes_accessed=4 * 2**20, transcendentals=0
        ),
    )(*arguments)
    return pl.pallas_call(
        finish,
        out_shape=(
            jax.ShapeDtypeStruct((1, ROWS, COLS), BF16),
            jax.ShapeDtypeStruct((ROWS, COLS), BF16),
            jax.ShapeDtypeStruct((COLS, RANK), F32),
        ),
        in_specs=[vmem] * 4,
        out_specs=(anywhere,) * 3,
        scratch_shapes=[
            pltpu.VMEM((COLS, RANK), F32),
            pltpu.VMEM((ROWS, COLS), BF16),
            pltpu.SemaphoreType.DMA((6,)),
        ],
        compiler_params=pltpu.CompilerParams(vmem_limit_bytes=40 * 2**20),
        cost_estimate=pl.CostEstimate(
            flops=2 * ROWS * COLS * RANK, bytes_accessed=3 * 2**20, transcendentals=0
        ),
    )(*made)


def solution(mesh):
    placed = (P("dp", "fsdp", "tensor"), P("dp", "fsdp", "tensor"), P("tensor", None))
    return jax.shard_map(
        shards,
        mesh=mesh,
        in_specs=placed,
        out_specs=(P("dp", "fsdp", "tensor"), P("fsdp", "tensor"), P("tensor", None)),
        check_vma=False,
    )
```

```python
import math

import jax
import jax.numpy as jnp
from jax import lax
from jax.experimental import pallas as pl
from jax.experimental.pallas import tpu as pltpu
from jax.sharding import PartitionSpec as P

D = 8192
FF = 14336
RANK = 128
MESH = pl.DeviceIdType.MESH
F32 = jnp.float32
BF16 = jnp.bfloat16

NZ = 16
ROWS = 512
HALF = 256
COLS = 896
XCH = 32
WCH = 64
GCH = 8
TILES = COLS // 128
PLACES = COLS // WCH
NB = 16

NEAR_Z = [4, 3, -3, 2, -2, 1, -1]
FAR_Z = sorted(range(1, NZ), key=lambda d: -min(d, NZ - d))
NEAR_XY = [(1, 1), (1, 3), (0, 2), (1, 0), (3, 0), (0, 1), (0, 3), (0, 0)]
FAR_XY = sorted(
    [(dx, dy) for dx in range(4) for dy in range(4) if (dx, dy) != (0, 0)],
    key=lambda o: -(min(o[0], 4 - o[0]) + min(o[1], 4 - o[1])),
)


def split3(a):
    high = a.astype(BF16)
    rest = a - high.astype(F32)
    mid = rest.astype(BF16)
    low = (rest - mid.astype(F32)).astype(BF16)
    return high, mid, low


def inverse_cholesky(a_ref, e_ref, panels):
    if panels[0] == 0:
        rows = lax.broadcasted_iota(jnp.int32, (RANK, RANK), 0)
        cols = lax.broadcasted_iota(jnp.int32, (RANK, RANK), 1)
        e_ref[...] = jnp.where(rows == cols, 1.0, 0.0).astype(F32)
    sub = lax.broadcasted_iota(jnp.int32, (NB, RANK), 0)

    def spread(t, j):
        return jnp.broadcast_to(t[j : j + 1, :], (NB, RANK))

    for base in [p * NB for p in panels]:
        last = base + NB
        xa = a_ref[base:last, :]
        xe = e_ref[base:last, :]
        col = [
            jnp.broadcast_to(xa[:, base + k : base + k + 1], (NB, RANK)) for k in range(NB)
        ]
        if last < RANK:
            c1, c2, c3 = split3(a_ref[last:, base:last])
            below = jnp.concatenate([c1, c1, c2, c1, c2, c3], 1)
        inverses = jnp.zeros((NB, RANK), F32)
        out = jnp.zeros((NB, RANK), F32)
        for j in range(NB):
            inv = 1.0 / spread(col[j], j)
            inverses = jnp.where(sub == j, inv, inverses)
            row_e = spread(xe, j)
            out = jnp.where(sub == j, row_e, out)
            factor = jnp.where(sub != j, col[j] * inv, 0.0)
            xa = xa - factor * spread(xa, j)
            xe = xe - factor * row_e
            for k in range(j + 1, NB):
                col[k] = col[k] - factor * spread(col[k], j)
        e_ref[base:last, :] = out * jnp.sqrt(inverses)
        if last < RANK:
            v1, v2, v3 = split3(jnp.concatenate([xa * inverses, xe * inverses], 1))
            solved = jnp.concatenate([v1, v2, v1, v3, v2, v1], 0)
            change = jnp.dot(below, solved, preferred_element_type=F32)
            a_ref[last:, :] = a_ref[last:, :] - change[:, :RANK]
            e_ref[last:, :] = e_ref[last:, :] - change[:, RANK:]


def right_times(tiles_ref, m, first=0, last=TILES):
    parts = jnp.concatenate(split3(m)[:2], 0)
    out = []
    for i in range(first, last):
        tile = tiles_ref[i * 128 : (i + 1) * 128, :]
        r = lax.dot_general(tile, parts, (((0,), (1,)), ((), ())), preferred_element_type=F32)
        out.append(r[:, :RANK] + r[:, RANK:])
    return out


def rows_times(x, m):
    parts = jnp.concatenate(split3(m)[:2], 0)
    r = lax.dot_general(x, parts, (((1,), (1,)), ((), ())), preferred_element_type=F32)
    return r[:, :RANK] + r[:, RANK:]


def kernel(
    mom, grad, fac, new_mom, right, ob, norm,
    m_v, g_v, f_v, fb, own, oth, xs0, xr0, xs1, xr1, xo, xp, xl, xoth, ws, wr, wo, wp, wa, gs, gr, go, gp0, gp1, ga,
    qs, qr0, qr1, lower, a_s, acc, tally, load, send, recv,
):
    c = lax.axis_index("dp")
    f = lax.axis_index("fsdp")
    t = lax.axis_index("tensor")
    x = f // 4
    y = lax.rem(f, 4)
    other = 1 - c
    partner = (other, f, t)

    def core(dc):
        return c if dc == 0 else other

    def along_z(d, dc=0):
        return (core(dc), f, lax.rem(t + d + NZ, NZ))

    def near_z(d, dc=0):
        return along_z(4 + 8 * lax.rem(t, 2) if d == 4 else d, dc)

    def along_xy(dx, dy, dc=0):
        return (core(dc), lax.rem(x + dx, 4) * 4 + lax.rem(y + dy, 4), t)

    def pair_of(chip):
        px = chip // 4
        return lax.rem(px, 2) * 4 + lax.rem(lax.rem(chip, 4) + 2 * (px // 2), 4)

    pair = pair_of(f)
    half = x // 2
    place = c * 8 + pair
    owner = place < PLACES
    idle = jnp.logical_not(owner)
    ring = [along_z(d) for d in FAR_Z]
    chips = [along_xy(*o) for o in FAR_XY]
    near = [(2 * (len(NEAR_XY) - 1 - i) + dc, along_xy(*o, dc)) for i, o in enumerate(NEAR_XY) for dc in (0, 1)]
    near = [(slot, to) for slot, to in near if slot]

    def chunk(index, size):
        return pl.ds(pl.multiple_of(index * size, size), size)

    def put(src, dst, phase, to, group=0):
        pltpu.make_async_remote_copy(
            src_ref=src, dst_ref=dst, send_sem=send.at[group], recv_sem=recv.at[phase],
            device_id=to, device_id_type=MESH,
        ).start()

    def got(region, phase):
        pltpu.make_async_remote_copy(
            src_ref=region, dst_ref=region, send_sem=send.at[0], recv_sem=recv.at[phase],
            device_id=partner, device_id_type=MESH,
        ).wait_recv()

    def all_sent(region, group):
        pltpu.make_async_remote_copy(
            src_ref=region, dst_ref=region, send_sem=send.at[group], recv_sem=recv.at[0],
            device_id=partner, device_id_type=MESH,
        ).wait_send()

    def summed(ref, it, size, count):
        total = ref[it, 0:size, :].astype(F32)
        for k in range(1, count):
            total = total + ref[it, k * size : (k + 1) * size, :].astype(F32)
        return total

    greet = [along_z(d, dc) for d in (4, -4) for dc in (0, 1)]
    greet += [along_xy(*o, dc) for o in FAR_XY[:5] for dc in (0, 1)]
    greet += [along_z(d, dc) for d in (3, -3, 2, -2, 1, -1) for dc in (0, 1)]
    greet += [along_xy(*o, dc) for o in FAR_XY[5:] for dc in (0, 1)] + [partner]
    barrier = pltpu.get_barrier_semaphore()

    def signal(some):
        for to in some:
            pl.semaphore_signal(barrier, inc=1, device_id=to, device_id_type=MESH)

    signal(greet[:14])
    load_f = pltpu.make_async_copy(fac, f_v, load.at[4])
    load_f.start()
    for i in range(4):
        r = pl.ds(i * 128, 128)
        pair_in = [
            pltpu.make_async_copy(mom.at[0, r], m_v.at[r], load.at[i]),
            pltpu.make_async_copy(grad.at[0, r], g_v.at[r], load.at[i]),
        ]
        for copy in pair_in:
            copy.start()
    signal(greet[14:])
    load_f.wait()
    fb[...] = f_v[...].astype(BF16)
    for i in range(4):
        both = tally.at[pl.ds(0, 2 * 128 * TILES)]
        pltpu.make_async_copy(both, both, load.at[i]).wait()
        r = pl.ds(i * 128, 128)
        block = (m_v[r, :].astype(F32) + g_v[r, :].astype(F32)).astype(BF16)
        own[r, :] = block
        xs0[r, :] = (0.5 * jnp.dot(block, fb[...], preferred_element_type=F32)).astype(BF16)

    mine = pl.ds(pl.multiple_of(c * HALF, HALF), HALF)
    theirs = pl.ds(pl.multiple_of(other * HALF, HALF), HALF)
    nt = (((1,), (1,)), ((), ()))
    tn = (((0,), (0,)), ((), ()))

    def phase(it, k):
        return 2 + 9 * it + k

    def left_spread(it, total):
        xo[it] = total.astype(BF16)
        for to in ring:
            put(xo.at[it], xp.at[it, chunk(t, XCH)], phase(it, 1), to)
        xp[it, chunk(t, XCH), :] = total.astype(BF16)

    def left_here(it):
        got(xp.at[it, pl.ds(0, (NZ - 1) * XCH)], phase(it, 1))
        both = xp[it, 0:HALF, :].astype(F32) + xp[it, HALF : 2 * HALF, :].astype(F32)
        return both.astype(BF16)

    def right_out(it, left):
        part = lax.dot_general(left, own[mine, :], tn, preferred_element_type=F32)
        part = part + lax.dot_general(left, oth[...], tn, preferred_element_type=F32)
        part = (0.5 * part).astype(BF16)
        for i in range(TILES):
            ws[it, i * 128 : (i + 1) * 128, :] = part[:, i * 128 : (i + 1) * 128]
        for slot, to in near:
            there = to[0] * 8 + pair_of(to[1])

            @pl.when(there < PLACES)
            def _():
                put(ws.at[it, chunk(there, WCH)], wr.at[it, pl.ds(slot * WCH, WCH)], phase(it, 2), to)

        @pl.when(owner)
        def _():
            wr[it, 0:WCH, :] = ws[it, chunk(place, WCH), :]

    def right_spread(it):
        @pl.when(owner)
        def _():
            got(wr.at[it, pl.ds(WCH, 15 * WCH)], phase(it, 2))
            total = summed(wr, it, WCH, 16).astype(BF16)
            wo[it] = total
            rows = chunk(half * 8 + pair, WCH)
            for to in chips:
                put(wo.at[it], wp.at[it, rows], phase(it, 3), to)
            wp[it, rows, :] = total

    def right_join(it):
        @pl.when(c == 0)
        def _():
            got(wp.at[it, pl.ds(0, 15 * WCH)], phase(it, 3))
            both = wp[it, 0:512, :].astype(F32) + wp[it, 512:1024, :].astype(F32)
            wa[it, 0:512, :] = both.astype(BF16)
            put(wa.at[it, pl.ds(0, 512)], wa.at[it, pl.ds(0, 512)], phase(it, 4), partner)

        @pl.when(c == 1)
        def _():
            @pl.when(owner)
            def _():
                got(wp.at[it, pl.ds(0, 11 * WCH)], phase(it, 3))

            @pl.when(idle)
            def _():
                got(wp.at[it, pl.ds(0, 12 * WCH)], phase(it, 3))

            both = wp[it, 0:384, :].astype(F32) + wp[it, 512:896, :].astype(F32)
            wa[it, 512:896, :] = both.astype(BF16)
            put(wa.at[it, pl.ds(512, 384)], wa.at[it, pl.ds(512, 384)], phase(it, 4), partner)

    def right_here(it):
        @pl.when(c == 0)
        def _():
            got(wa.at[it, pl.ds(512, 384)], phase(it, 4))

        @pl.when(c == 1)
        def _():
            got(wa.at[it, pl.ds(0, 512)], phase(it, 4))

    def gram_out(it, left):
        gs[it] = lax.dot_general(left, left, tn, preferred_element_type=F32)
        for slot, to in near:
            there = to[0] * 8 + pair_of(to[1])
            put(gs.at[it, chunk(there, GCH)], gr.at[it, pl.ds(slot * GCH, GCH)], phase(it, 5), to)
        gr[it, 0:GCH, :] = gs[it, chunk(place, GCH), :]

    def gram_owned(it):
        got(gr.at[it, pl.ds(GCH, 15 * GCH)], phase(it, 5))
        total = summed(gr, it, GCH, 16)
        go[it] = total
        return total

    def gram_spread_core(total):
        rows = chunk(half * 8 + pair, GCH)
        for to in chips:
            put(go.at[0], gp0.at[0, rows], phase(0, 6), to)
        gp0[0, rows, :] = total

    def gram_join_core():
        got(gp0.at[0, pl.ds(0, 15 * GCH)], phase(0, 6))
        rows = chunk(c, RANK // 2)
        ga[rows, :] = gp0[0, 0 : RANK // 2, :] + gp0[0, RANK // 2 : RANK, :]
        put(ga.at[rows], ga.at[rows], phase(0, 8), partner)
        got(ga.at[pl.ds(0, RANK // 2)], phase(0, 8))
        return ga[...]

    def gram_spread_all(total):
        rows = chunk(half * 16 + place, GCH)
        for o in FAR_XY:
            for dc in (0, 1):
                put(go.at[1], gp1.at[0, rows], phase(1, 6), along_xy(*o, dc))
        put(go.at[1], gp1.at[0, rows], phase(1, 6), partner)
        gp1[0, rows, :] = total

    def gram_join_all():
        got(gp1.at[0, pl.ds(0, 31 * GCH)], phase(1, 6))
        return gp1[0, 0:RANK, :] + gp1[0, RANK : 2 * RANK, :]

    def squares_sum(it, tiles):
        total = jnp.sum(tiles[0] * tiles[0], axis=0, keepdims=True)
        for tile in tiles[1:]:
            total = total + jnp.sum(tile * tile, axis=0, keepdims=True)
        qs[it] = total

    def squares_send_core():
        for to in ring:
            put(qs.at[0], qr0.at[t], phase(0, 7), to, 1)
        qr0[t] = qs[0]

    def squares_send_all():
        slot = 2 * t + c
        for d in FAR_Z:
            for dc in (0, 1):
                put(qs.at[1], qr1.at[slot], phase(1, 7), along_z(d, dc), 2)
        put(qs.at[1], qr1.at[slot], phase(1, 7), partner, 2)
        qr1[slot] = qs[1]

    def norms(it):
        ref, count = (qr0, NZ) if it == 0 else (qr1, 2 * NZ)
        got(ref.at[pl.ds(0, count - 1)], phase(it, 7))
        total = ref[0]
        for k in range(1, count):
            total = total + ref[k]
        return jnp.sqrt(total + 1e-06)

    pl.semaphore_wait(barrier, len(greet))
    for d in NEAR_Z + [0]:
        for dc in (0, 1):
            if (d, dc) == (0, 0):
                continue
            to = near_z(d, dc)
            src = xs0.at[chunk(to[0] * 8 + lax.rem(to[2], 8), XCH)]
            put(src, xr0.at[0, pl.ds((2 * (d % 8) + dc) * XCH, XCH)], phase(0, 0), to)
    xr0[0, 0:XCH, :] = xs0[chunk(c * 8 + lax.rem(t, 8), XCH), :]
    got(xr0.at[0, pl.ds(XCH, 15 * XCH)], phase(0, 0))
    left_spread(0, summed(xr0, 0, XCH, 16))
    put(own.at[theirs], oth, 0, partner)
    got(oth, 0)
    left = left_here(0)
    right_out(0, left)
    gram_out(0, left)
    right_spread(0)
    gram_spread_core(gram_owned(0))
    right_join(0)

    def products(first, last):
        tiles = [wa[0, i * 128 : (i + 1) * 128, :] for i in range(first, last)]
        tiles = jnp.concatenate(tiles, 1)
        cols = pl.ds(first * 128, (last - first) * 128)
        part = lax.dot_general(own[mine, cols], tiles, nt, preferred_element_type=F32)
        return part + lax.dot_general(oth[:, cols], tiles, nt, preferred_element_type=F32)

    @pl.when(c == 0)
    def _():
        acc[...] = products(0, 4)

    @pl.when(c == 1)
    def _():
        acc[...] = products(4, 7)

    right_here(0)

    @pl.when(c == 0)
    def _():
        xs1[0] = (0.5 * (acc[...] + products(4, 7))).astype(BF16)

    @pl.when(c == 1)
    def _():
        xs1[0] = (0.5 * (acc[...] + products(0, 4))).astype(BF16)

    for d in NEAR_Z:
        to = near_z(d)
        src = xs1.at[0, chunk(lax.rem(to[2], 8), XCH)]
        put(src, xr1.at[0, pl.ds((d % 8) * XCH, XCH)], phase(1, 0), to)
    xr1[0, 0:XCH, :] = xs1[0, chunk(lax.rem(t, 8), XCH), :]
    a_s[...] = gram_join_core()
    inverse_cholesky(a_s, lower.at[0], range(8))
    low_parts = split3(lower[0])
    low_parts = jnp.concatenate([low_parts[0], low_parts[1], low_parts[0]], 1)
    got(xr1.at[0, pl.ds(XCH, 7 * XCH)], phase(1, 0))
    owned = split3(summed(xr1, 0, XCH, 8))
    owned = jnp.concatenate([owned[0], owned[0], owned[1]], 1)
    left_spread(1, lax.dot_general(owned, low_parts, nt, preferred_element_type=F32))
    squares_sum(0, right_times(wa.at[0], lower[0]))
    squares_send_core()
    left = left_here(1)
    gram_out(1, left)
    xl[...] = left
    put(xl, xoth, 1, partner)
    right_out(1, left)
    scale = jnp.broadcast_to(1.0 / norms(0), (RANK, RANK))
    a_s[...] = scale * scale.T
    gram_spread_all(gram_owned(1))
    right_spread(1)
    a_s[...] = gram_join_all() * a_s[...]
    inverse_cholesky(a_s, lower.at[1], range(8))
    mix = lower[1] * scale
    right_join(1)

    def right_tiles(first, last):
        tiles = right_times(wa.at[1], mix, first, last)
        for i in range(first, last):
            right[i * 128 : (i + 1) * 128, :] = tiles[i - first]
        return tiles

    @pl.when(c == 0)
    def _():
        squares_sum(1, right_tiles(0, 4))

    @pl.when(c == 1)
    def _():
        squares_sum(1, right_tiles(4, 7))

    squares_send_all()
    right_here(1)

    @pl.when(c == 0)
    def _():
        right_tiles(4, 7)

    @pl.when(c == 1)
    def _():
        right_tiles(0, 4)

    got(xoth, 1)
    ob[mine, :] = rows_times(xl[...], mix).astype(BF16)
    ob[theirs, :] = rows_times(xoth[...], mix).astype(BF16)
    right_b = right[...].astype(BF16)
    for i in range(4):
        r = pl.ds(i * 128, 128)
        feedback = lax.dot_general(ob[r, :], right_b, nt, preferred_element_type=F32)
        new_mom[0, r, :] = (own[r, :].astype(F32) - 0.05 * feedback).astype(BF16)

    all_sent(qr0.at[pl.ds(0, NZ - 1)], 1)
    all_sent(qr1.at[pl.ds(0, 2 * NZ - 1)], 2)
    everyone = 1792 + 256 + 480 + 224 + 2 * 480 + 2 * 240 + 240 + 496 + 128

    @pl.when(c == 0)
    def _():
        all_sent(tally.at[pl.ds(0, everyone + 2 * (13 * WCH + 15 * WCH + 512))], 0)

    @pl.when((c == 1) & owner)
    def _():
        all_sent(tally.at[pl.ds(0, everyone + 2 * (13 * WCH + 15 * WCH + 384))], 0)

    @pl.when(idle)
    def _():
        all_sent(tally.at[pl.ds(0, everyone + 2 * (14 * WCH + 384))], 0)

    norm[...] = jnp.broadcast_to(1.0 / norms(1), (8, RANK))


def finish(new_mom, right, ob, norm, new_mom_out, update, new_fac, fac, up, sem):
    first = pltpu.make_async_copy(new_mom, new_mom_out, sem.at[0])
    first.start()
    fac[...] = right[...] * norm[0:1, :]
    copies = [first, pltpu.make_async_copy(fac, new_fac, sem.at[1])]
    copies[1].start()
    factor_b = fac[...].astype(BF16)
    nt = (((1,), (1,)), ((), ()))
    for i in range(4):
        r = pl.ds(i * 128, 128)
        low_rank = lax.dot_general(ob[r, :], factor_b, nt, preferred_element_type=F32)
        up[r, :] = (math.sqrt(D * FF / RANK) * low_rank).astype(BF16)
        copy = pltpu.make_async_copy(up.at[r], update.at[r], sem.at[2 + i])
        copy.start()
        copies.append(copy)
    for copy in copies:
        copy.wait()


def shards(momentum, gradient, right_factor):
    scratch = [
        pltpu.VMEM((ROWS, COLS), BF16),
        pltpu.VMEM((ROWS, COLS), BF16),
        pltpu.VMEM((COLS, RANK), F32),
        pltpu.VMEM((COLS, RANK), BF16),
        pltpu.VMEM((ROWS, COLS), BF16),
        pltpu.VMEM((HALF, COLS), BF16),
        pltpu.VMEM((ROWS, RANK), BF16),
        pltpu.VMEM((1, 16 * XCH, RANK), BF16),
        pltpu.VMEM((1, HALF, RANK), BF16),
        pltpu.VMEM((1, 8 * XCH, RANK), BF16),
        pltpu.VMEM((2, XCH, RANK), BF16),
        pltpu.VMEM((2, NZ * XCH, RANK), BF16),
        pltpu.VMEM((HALF, RANK), BF16),
        pltpu.VMEM((HALF, RANK), BF16),
        pltpu.VMEM((2, COLS, RANK), BF16),
        pltpu.VMEM((2, 16 * WCH, RANK), BF16),
        pltpu.VMEM((2, WCH, RANK), BF16),
        pltpu.VMEM((2, 16 * WCH, RANK), BF16),
        pltpu.VMEM((2, COLS, RANK), BF16),
        pltpu.VMEM((2, RANK, RANK), F32),
        pltpu.VMEM((2, 16 * GCH, RANK), F32),
        pltpu.VMEM((2, GCH, RANK), F32),
        pltpu.VMEM((1, 16 * GCH, RANK), F32),
        pltpu.VMEM((1, 32 * GCH, RANK), F32),
        pltpu.VMEM((RANK, RANK), F32),
        pltpu.VMEM((2, 1, RANK), F32),
        pltpu.VMEM((NZ, 1, RANK), F32),
        pltpu.VMEM((2 * NZ, 1, RANK), F32),
        pltpu.VMEM((2, RANK, RANK), F32),
        pltpu.VMEM((RANK, RANK), F32),
        pltpu.VMEM((HALF, RANK), F32),
        pltpu.VMEM((10400, RANK), BF16),
        pltpu.SemaphoreType.DMA((5,)),
        pltpu.SemaphoreType.DMA((3,)),
        pltpu.SemaphoreType.DMA((20,)),
    ]
    arguments = [
        pltpu.with_memory_space_constraint(v, pltpu.HBM)
        for v in (momentum, gradient, right_factor)
    ]
    vmem = pl.BlockSpec(memory_space=pltpu.VMEM)
    anywhere = pl.BlockSpec(memory_space=pl.ANY)
    made = pl.pallas_call(
        kernel,
        out_shape=(
            jax.ShapeDtypeStruct((1, ROWS, COLS), BF16),
            jax.ShapeDtypeStruct((COLS, RANK), F32),
            jax.ShapeDtypeStruct((ROWS, RANK), BF16),
            jax.ShapeDtypeStruct((8, RANK), F32),
        ),
        in_specs=[anywhere] * 3,
        out_specs=(vmem,) * 4,
        scratch_shapes=scratch,
        compiler_params=pltpu.CompilerParams(
            collective_id=0, has_side_effects=True, vmem_limit_bytes=40 * 2**20
        ),
        cost_estimate=pl.CostEstimate(
            flops=10 * ROWS * COLS * RANK, bytes_accessed=4 * 2**20, transcendentals=0
        ),
    )(*arguments)
    return pl.pallas_call(
        finish,
        out_shape=(
            jax.ShapeDtypeStruct((1, ROWS, COLS), BF16),
            jax.ShapeDtypeStruct((ROWS, COLS), BF16),
            jax.ShapeDtypeStruct((COLS, RANK), F32),
        ),
        in_specs=[vmem] * 4,
        out_specs=(anywhere,) * 3,
        scratch_shapes=[
            pltpu.VMEM((COLS, RANK), F32),
            pltpu.VMEM((ROWS, COLS), BF16),
            pltpu.SemaphoreType.DMA((6,)),
        ],
        compiler_params=pltpu.CompilerParams(vmem_limit_bytes=40 * 2**20),
        cost_estimate=pl.CostEstimate(
            flops=2 * ROWS * COLS * RANK, bytes_accessed=3 * 2**20, transcendentals=0
        ),
    )(*made)


def solution(mesh):
    placed = (P("dp", "fsdp", "tensor"), P("dp", "fsdp", "tensor"), P("tensor", None))
    return jax.shard_map(
        shards,
        mesh=mesh,
        in_specs=placed,
        out_specs=(P("dp", "fsdp", "tensor"), P("fsdp", "tensor"), P("tensor", None)),
        check_vma=False,
    )
```
